128 devices in a mesh: seq: 128 (over z, y, x, core).
Axes of the slice: x: 4, y: 4, z: 4, core: 2. Of those that a mesh axis runs over, the one named last changes fastest.
Arguments:
- query_points: bfloat16 [65536, 512], P('seq'), may hold values from -6 to 6
- key_points: bfloat16 [65536, 512], P('seq'), may hold values from -6 to 6
- value_points: bfloat16 [65536, 512], P('seq'), may hold values from -6 to 6
- cotangent: bfloat16 [65536, 512], P('seq'), may hold values from -6 to 6
- hilbert_order: int32 [65536], P('seq'), may hold values from 0 to 65535, as said below
Outputs:
- attended: bfloat16 [65536, 512], P('seq')
- query_grad: bfloat16 [65536, 512], P('seq')
- key_grad: bfloat16 [65536, 512], P('seq')
- value_grad: bfloat16 [65536, 512], P('seq')
The draws below stay inside these ranges and needn't reach their ends.
Inputs may be any that keep to these rules, and one draw needn't show every extreme that they name: `hilbert_order`: within each aligned block of 512 positions, the entries are a permutation of that block's own indices.
All inputs are finite; a program needn't handle non-finite values.
Results may differ from the reference program's by a relative error of at most 0.012.
The reference program's roundings to bfloat16 on the way count: a program that leaves them out, or rounds other values in their place, can miss the bound.
Values may be sent and summed in bfloat16 or wider, within the bound.
A program may use at most 128 MiB of HBM per device.

```python
import jax
import jax.numpy as jnp
from jax import lax

HEADS = 8
HEAD_DIM = 64
FEAT = 512
BLOCK_ROWS = 128
POOL = 4
TOK_DEV = 512
TOKENS = 65536


def hilbert_blocks(key):
    blocks = TOKENS // TOK_DEV
    keys = jax.random.split(jax.random.fold_in(key, 11), blocks)
    local = jax.vmap(lambda single: jax.random.permutation(single, TOK_DEV))(keys)
    offsets = jnp.arange(blocks, dtype=jnp.int32)[:, None] * TOK_DEV
    return (local.astype(jnp.int32) + offsets).reshape(TOKENS)


def draw_hilbert_order(key, part):
    return hilbert_blocks(key)


def draw_query_points(key, part):
    order = hilbert_blocks(key)
    key = jax.random.fold_in(key, 1)
    base = jnp.clip(jax.random.normal(key, (TOKENS, FEAT), jnp.float32), -6.0, 6.0)
    return jnp.zeros((TOKENS, FEAT), jnp.float32).at[order].set(base).astype(jnp.bfloat16)


def draw_key_points(key, part):
    order = hilbert_blocks(key)
    key = jax.random.fold_in(key, 2)
    base = jnp.clip(jax.random.normal(key, (TOKENS, FEAT), jnp.float32), -6.0, 6.0)
    return jnp.zeros((TOKENS, FEAT), jnp.float32).at[order].set(base).astype(jnp.bfloat16)


def block_levels(own_key, shape, cuts, least, largest):
    factor_of = 1.0
    for position, shards_of in cuts:
        steps = jax.random.uniform(jax.random.fold_in(jax.random.fold_in(own_key, 6), position), (shards_of,), jnp.float32, least / len(cuts), largest / len(cuts))
        factor_of = factor_of * jnp.repeat(jnp.exp(steps), shape[position] // shards_of).reshape((-1,) + (1,) * (len(shape) - 1 - position))
    return factor_of


def gaussian(stream_key, shape, deviation, limit, cuts=(), held_as=jnp.bfloat16):
    factor_of = block_levels(stream_key, shape, cuts, -0.22, 0.18) if cuts else 1.0
    values = jax.random.normal(stream_key, shape, jnp.float32) * deviation * factor_of
    return jnp.minimum(jnp.maximum(values, -limit), limit).astype(held_as)


def setup_inputs(seed: int = 0) -> dict:
    key_of = jax.random.split(jax.random.key(seed), 6)
    query_points = draw_query_points(jax.random.fold_in(key_of[5], 71), 0)
    key_points = draw_key_points(jax.random.fold_in(key_of[5], 71), 0)
    value_points = gaussian(key_of[2], (TOKENS, FEAT), 1.0, 6.0, ((0, 128),))
    cotangent = gaussian(key_of[3], (TOKENS, FEAT), 1.0, 6.0, ((0, 128),))
    hilbert_order = draw_hilbert_order(jax.random.fold_in(key_of[5], 71), 0)
    return {"query_points": query_points, "key_points": key_points, "value_points": value_points, "cotangent": cotangent, "hilbert_order": hilbert_order}


NEG = -1.0e30


def to_bf16(value_rows):
    return lax.optimization_barrier(value_rows.astype(jnp.bfloat16))


def split_heads(value_rows):
    return value_rows.reshape(value_rows.shape[:-1] + (HEADS, HEAD_DIM))


def pooled(rows, factor, average):
    if factor == 1:
        return rows
    grouped = jnp.sum(rows.astype(jnp.float32).reshape(rows.shape[0] // factor, factor, rows.shape[1]), axis=1)
    if average:
        grouped = grouped / factor
    return to_bf16(grouped)


def permitted(qpos, kpos, level, count):
    upper = qpos[:, None]
    lower = kpos[None, :]
    inside = (lower >= 0) & (lower < count) & (upper >= 0) & (upper < count)
    near = jnp.abs(upper // BLOCK_ROWS - lower // BLOCK_ROWS) <= 1
    if level > 0:
        width = BLOCK_ROWS // POOL
        near = near & (jnp.abs(upper // width - lower // width) > 1)
    return inside & near


def scores_of(query, keys, allow):
    raw = jnp.einsum("qhd,khd->hqk", split_heads(query).astype(jnp.float32), split_heads(keys).astype(jnp.float32))
    return jnp.where(allow[None], raw * HEAD_DIM ** -0.5, NEG)


def row_padding(value_rows):
    return jnp.pad(value_rows, ((BLOCK_ROWS, BLOCK_ROWS), (0, 0)))


def level_forward(qc, kc, value_coarse, level):
    count = qc.shape[0]
    factor = POOL ** level
    kpad = row_padding(kc)
    value_padded = row_padding(value_coarse)

    def block(number):
        start_index = number * BLOCK_ROWS
        query = lax.dynamic_slice_in_dim(qc, start_index, BLOCK_ROWS, 0)
        keys = lax.dynamic_slice_in_dim(kpad, start_index, 3 * BLOCK_ROWS, 0)
        value_rows = lax.dynamic_slice_in_dim(value_padded, start_index, 3 * BLOCK_ROWS, 0)
        qpos = start_index + jnp.arange(BLOCK_ROWS, dtype=jnp.int32)
        kpos = start_index - BLOCK_ROWS + jnp.arange(3 * BLOCK_ROWS, dtype=jnp.int32)
        scores = scores_of(query, keys, permitted(qpos, kpos, level, count))
        top = jnp.max(scores, axis=2)
        weights = jnp.exp(scores - top[:, :, None])
        numer = jnp.einsum("hqk,khd->qhd", to_bf16(weights).astype(jnp.float32), split_heads(value_rows).astype(jnp.float32))
        return numer.reshape(BLOCK_ROWS, -1), factor * jnp.sum(weights, axis=2).T, top.T

    numer, total, top = lax.map(block, jnp.arange(count // BLOCK_ROWS, dtype=jnp.int32))
    return numer.reshape(count, -1), total.reshape(count, HEADS), top.reshape(count, HEADS)


def level_query_grads(qc, kc, value_coarse, top, gsum, esum, level):
    count = qc.shape[0]
    factor = POOL ** level
    kpad = row_padding(kc)
    value_padded = row_padding(value_coarse)

    def block(number):
        start_index = number * BLOCK_ROWS
        query = lax.dynamic_slice_in_dim(qc, start_index, BLOCK_ROWS, 0)
        keys = lax.dynamic_slice_in_dim(kpad, start_index, 3 * BLOCK_ROWS, 0)
        value_rows = lax.dynamic_slice_in_dim(value_padded, start_index, 3 * BLOCK_ROWS, 0)
        qpos = start_index + jnp.arange(BLOCK_ROWS, dtype=jnp.int32)
        kpos = start_index - BLOCK_ROWS + jnp.arange(3 * BLOCK_ROWS, dtype=jnp.int32)
        scores = scores_of(query, keys, permitted(qpos, kpos, level, count))
        tops = lax.dynamic_slice_in_dim(top, start_index, BLOCK_ROWS, 0)
        weights = jnp.exp(scores - tops.T[:, :, None])
        grad_rows = lax.dynamic_slice_in_dim(gsum, start_index, BLOCK_ROWS, 0)
        e_rows = lax.dynamic_slice_in_dim(esum, start_index, BLOCK_ROWS, 0)
        mixing = jnp.einsum("qhd,khd->hqk", split_heads(grad_rows).astype(jnp.float32), split_heads(value_rows).astype(jnp.float32))
        dscore = to_bf16(weights * (mixing - factor * e_rows.T[:, :, None])).astype(jnp.float32)
        grads = HEAD_DIM ** -0.5 * jnp.einsum("hqk,khd->qhd", dscore, split_heads(keys).astype(jnp.float32))
        return grads.reshape(BLOCK_ROWS, -1)

    return lax.map(block, jnp.arange(count // BLOCK_ROWS, dtype=jnp.int32)).reshape(count, -1)


def level_key_grads(qc, kc, value_coarse, top, gsum, esum, level):
    count = qc.shape[0]
    factor = POOL ** level
    qpad = row_padding(qc)
    gpad = row_padding(gsum)
    tpad = row_padding(top)
    epad = row_padding(esum)

    def block(number):
        start_index = number * BLOCK_ROWS
        keys = lax.dynamic_slice_in_dim(kc, start_index, BLOCK_ROWS, 0)
        value_rows = lax.dynamic_slice_in_dim(value_coarse, start_index, BLOCK_ROWS, 0)
        query = lax.dynamic_slice_in_dim(qpad, start_index, 3 * BLOCK_ROWS, 0)
        grad_rows = lax.dynamic_slice_in_dim(gpad, start_index, 3 * BLOCK_ROWS, 0)
        tops = lax.dynamic_slice_in_dim(tpad, start_index, 3 * BLOCK_ROWS, 0)
        e_rows = lax.dynamic_slice_in_dim(epad, start_index, 3 * BLOCK_ROWS, 0)
        qpos = start_index - BLOCK_ROWS + jnp.arange(3 * BLOCK_ROWS, dtype=jnp.int32)
        kpos = start_index + jnp.arange(BLOCK_ROWS, dtype=jnp.int32)
        scores = scores_of(query, keys, permitted(qpos, kpos, level, count))
        weights = jnp.exp(scores - tops.T[:, :, None])
        grads32 = split_heads(grad_rows).astype(jnp.float32)
        value_terms = jnp.einsum("hqk,qhd->khd", to_bf16(weights).astype(jnp.float32), grads32)
        mixing = jnp.einsum("qhd,khd->hqk", grads32, split_heads(value_rows).astype(jnp.float32))
        dscore = to_bf16(weights * (mixing - factor * e_rows.T[:, :, None])).astype(jnp.float32)
        key_terms = HEAD_DIM ** -0.5 * jnp.einsum("hqk,qhd->khd", dscore, split_heads(query).astype(jnp.float32))
        return key_terms.reshape(BLOCK_ROWS, -1), value_terms.reshape(BLOCK_ROWS, -1)

    key_terms, value_terms = lax.map(block, jnp.arange(count // BLOCK_ROWS, dtype=jnp.int32))
    return key_terms.reshape(count, -1), value_terms.reshape(count, -1)


def reference(query_points, key_points, value_points, cotangent, hilbert_order):
    q_fine = query_points[hilbert_order]
    finest_keys = key_points[hilbert_order]
    v_fine = value_points[hilbert_order]
    dz_fine = cotangent[hilbert_order]
    stats = []
    for level in range(3):
        factor = POOL ** level
        qc = pooled(q_fine, factor, True)
        kc = pooled(finest_keys, factor, True)
        value_coarse = pooled(v_fine, factor, False)
        numer, total, top = level_forward(qc, kc, value_coarse, level)
        stats.append((factor, qc, kc, value_coarse, numer, total, top))
    tops = [jnp.repeat(item[6], item[0], axis=0) for item in stats]
    best = jnp.maximum(jnp.maximum(tops[0], tops[1]), tops[2])
    scales = [jnp.exp(top - best) for top in tops]
    denom = scales[0] * jnp.repeat(stats[0][5], stats[0][0], axis=0)
    denom = denom + scales[1] * jnp.repeat(stats[1][5], stats[1][0], axis=0)
    denom = denom + scales[2] * jnp.repeat(stats[2][5], stats[2][0], axis=0)
    mixed = scales[0][..., None] * split_heads(jnp.repeat(stats[0][4], stats[0][0], axis=0))
    mixed = mixed + scales[1][..., None] * split_heads(jnp.repeat(stats[1][4], stats[1][0], axis=0))
    mixed = mixed + scales[2][..., None] * split_heads(jnp.repeat(stats[2][4], stats[2][0], axis=0))
    mixed = mixed / denom[..., None]
    upstream = split_heads(dz_fine.astype(jnp.float32))
    delta = jnp.sum(upstream * mixed, axis=2)
    rows = q_fine.shape[0]
    query_sum = jnp.zeros((rows, FEAT), jnp.float32)
    key_sum = jnp.zeros((rows, FEAT), jnp.float32)
    value_sum = jnp.zeros((rows, FEAT), jnp.float32)
    for level in range(3):
        factor, qc, kc, value_coarse, numer, total, top = stats[level]
        count = rows // factor
        share = scales[level] / denom
        gsum = to_bf16(jnp.sum((share[..., None] * upstream).reshape(count, factor, FEAT), axis=1))
        esum = jnp.sum((share * delta).reshape(count, factor, HEADS), axis=1)
        dq = level_query_grads(qc, kc, value_coarse, top, gsum, esum, level)
        dk, dv = level_key_grads(qc, kc, value_coarse, top, gsum, esum, level)
        query_sum = query_sum + jnp.repeat(dq, factor, axis=0) / factor
        key_sum = key_sum + jnp.repeat(dk, factor, axis=0) / factor
        value_sum = value_sum + jnp.repeat(dv, factor, axis=0)
    outputs = []
    for value_rows in (mixed.reshape(rows, FEAT), query_sum, key_sum, value_sum):
        rounded = value_rows.astype(jnp.bfloat16)
        outputs.append(jnp.zeros_like(rounded).at[hilbert_order].set(rounded))
    return (outputs[0], outputs[1], outputs[2], outputs[3])
```

```python
import functools

import jax
import jax.numpy as jnp
from jax import lax
from jax.experimental import pallas as pl
from jax.experimental.pallas import tpu as pltpu
from jax.sharding import PartitionSpec as P

HEADS = 8
HEAD_DIM = 64
FEAT = 512
BLK = 128
ROWS = 512
SCALE = HEAD_DIM**-0.5
NEG = -1e30
MESH = pl.DeviceIdType.MESH
F32 = jnp.float32
BF16 = jnp.bfloat16

POS = {1: 0, 2: 1, 0: 2, 3: 4}
LEVEL1 = 3
WINDOW = {0: 128, 1: 256, 2: 0, 3: 768, 4: 384}
OWN1 = 768 + BLK
SLOTS = 10
WIN2 = 384


def nn(a, b):
    return lax.dot_general(a, b, (((1,), (0,)), ((), ())), preferred_element_type=F32)


def nt(a, b):
    return lax.dot_general(a, b, (((1,), (1,)), ((), ())), preferred_element_type=F32)


def iota(shape, dim):
    return lax.broadcasted_iota(jnp.int32, shape, dim)


def onehot(mask):
    return jnp.where(mask, 1.0, 0.0).astype(BF16)


def parts_of(x, count):
    parts = []
    for _ in range(count):
        part = x.astype(BF16)
        parts.append(part)
        x = x - part.astype(F32)
    return parts


def spread(x, matrix, count):
    total = None
    for part in parts_of(x, count):
        term = nn(part, matrix)
        total = term if total is None else total + term
    return total


def two_heads(x):
    zero = jnp.zeros((HEAD_DIM, x.shape[1]), x.dtype)
    upper = jnp.concatenate([x[:HEAD_DIM], zero], axis=1)
    lower = jnp.concatenate([zero, x[HEAD_DIM:]], axis=1)
    return jnp.concatenate([upper, lower], axis=0)


def own_blocks(x):
    return jnp.concatenate([x[:HEAD_DIM, :BLK], x[HEAD_DIM:, BLK:]], axis=0)


def kernel(
    n,
    order_ref,
    q_ref,
    k_ref,
    v_ref,
    dz_ref,
    out_ref,
    dq_out,
    dk_out,
    dv_out,
    place,
    pool1,
    pool1t,
    pool2,
    pool2t,
    kv,
    kvt,
    kv2own,
    kv2,
    kv2t,
    qg,
    halo_qg,
    stats,
    halo_stats,
    dzt,
    weights,
    sums,
    numer,
    q2m,
    g2m,
    k2m,
    v2m,
    weights2,
    numer2,
    g2own,
    g2win,
    bias1,
    bias2,
    share,
    delta,
    mixed,
    dqt,
    dq2,
    dkv,
    nb_send,
    nb_recv,
    l2_send,
    l2_recv,
):
    me = lax.axis_index("seq")
    left = lax.rem(me + n - 1, n)
    right = lax.rem(me + 1, n)
    core = lax.rem(me, 2)
    half = lax.rem(me // 2, 2)
    base = 4 * (me // 4 - 1)
    sibling = me + 1 - 2 * core
    chips = [0, 1, 3 - half, 4, 5]
    peers = [lax.rem(base + 2 * chip + core + n, n) for chip in chips]
    far_dense = [half + 3, half + 3, 2, half, half]

    barrier = pltpu.get_barrier_semaphore()
    for device in [left, right] + peers:
        pl.semaphore_signal(barrier, inc=1, device_id=(device,), device_id_type=MESH)

    def remote(src, dst, send, recv, device):
        return pltpu.make_async_remote_copy(
            src_ref=src,
            dst_ref=dst,
            send_sem=send,
            recv_sem=recv,
            device_id=(device,),
            device_id_type=MESH,
        )

    def kv0_copy(side):
        src, dst, to = [(512, 0, right), (128, 640, left)][side]
        return remote(
            kv.at[:, pl.ds(src, BLK)], kv.at[:, pl.ds(dst, BLK)],
            nb_send.at[side, 0], nb_recv.at[side, 0], to,
        )

    def kv1_copy(side):
        dst, to = [(768, right), (1024, left)][side]
        return remote(
            kv.at[:, pl.ds(OWN1, BLK)], kv.at[:, pl.ds(dst, BLK)],
            nb_send.at[side, 1], nb_recv.at[side, 1], to,
        )

    def qg_copy(side, which):
        src, to = [(3, right), (2, left)][side]
        return remote(
            qg.at[which, pl.ds(src, 2)], halo_qg.at[side, which],
            nb_send.at[side, 2 + which], nb_recv.at[side, 2 + which], to,
        )

    def stats_copy(side):
        src, to = [(3, right), (2, left)][side]
        return remote(
            stats.at[:, pl.ds(src, 2)], halo_stats.at[side],
            nb_send.at[side, 4], nb_recv.at[side, 4], to,
        )

    def slot_rows(slot):
        return pl.ds(pl.multiple_of(32 * slot, 32), 32)

    def far_refs(phase, slot):
        if phase == 0:
            return kv2own, kv2.at[:, slot_rows(slot)]
        return g2own, g2win.at[slot_rows(slot)]

    def direct_copy(phase, j):
        slot = 2 * far_dense[j] + core
        src, dst = far_refs(phase, slot)
        return remote(src, dst, l2_send.at[phase, j], l2_recv.at[phase, slot], peers[j])

    def arrival(phase, slot):
        src, dst = far_refs(phase, slot)
        return remote(src, dst, l2_send.at[phase, 0], l2_recv.at[phase, slot], sibling)

    def relay_copy(phase, j):
        slot = 2 * j + core
        _, dst = far_refs(phase, slot)
        return remote(dst, dst, l2_send.at[phase, 5 + j], l2_recv.at[phase, slot], sibling)

    order = order_ref[...] - me * ROWS
    place[...] = onehot(iota((ROWS, ROWS), 0) == order)
    column = jnp.transpose(jnp.broadcast_to(order.astype(F32), (BLK, ROWS)))
    lane = iota((ROWS, BLK), 1).astype(F32)
    gather = jnp.concatenate(
        [jnp.where(column == lane + float(BLK * i), 1.0, 0.0).astype(BF16) for i in range(4)], axis=1
    )
    pool1[...] = onehot(iota((BLK, ROWS), 0) == (iota((BLK, ROWS), 1) >> 2))
    pool1t[...] = onehot((iota((ROWS, BLK), 0) >> 2) == iota((ROWS, BLK), 1))
    pool2[...] = onehot((iota((256, ROWS), 0) & 31) == (iota((256, ROWS), 1) >> 4))
    pool2t[...] = onehot((iota((ROWS, 256), 0) >> 4) == (iota((ROWS, 256), 1) & 31))

    kv[0, 128:640] = nn(gather, k_ref[...]).astype(BF16)
    kv[1, 128:640] = nn(gather, v_ref[...]).astype(BF16)
    pl.semaphore_wait(barrier, 7)
    for side in range(2):
        kv0_copy(side).start()
    pooled_k = nn(pool2[0:32], kv[0, 128:640])
    pooled_v = nn(pool2[0:32], kv[1, 128:640])
    kv2own[0] = (pooled_k * (1.0 / 16)).astype(BF16)
    kv2own[1] = pooled_v.astype(BF16)
    query = (nn(gather, q_ref[...]) * SCALE).astype(BF16)
    kv2own[2] = (nn(pool2[0:32], query) * (1.0 / 16)).astype(BF16)
    for j in range(5):
        direct_copy(0, j).start()
    kv[0, OWN1 : OWN1 + BLK] = (nn(pool1[...], kv[0, 128:640]) * 0.25).astype(BF16)
    kv[1, OWN1 : OWN1 + BLK] = nn(pool1[...], kv[1, 128:640]).astype(BF16)
    for side in range(2):
        kv1_copy(side).start()
    query_t = jnp.transpose(query)
    for b in range(4):
        qg[0, POS[b]] = query_t[:, BLK * b : BLK * (b + 1)]
    qg[0, LEVEL1] = (nn(query_t, pool1t[...]) * 0.25).astype(BF16)
    for side in range(2):
        qg_copy(side, 0).start()

    head_lane = (iota((FEAT, 256), 0) >> 6) == (iota((FEAT, 256), 1) >> 5)
    q2m[...] = jnp.where(head_lane, nn(query_t, pool2t[...]) * (1.0 / 16), 0.0).astype(BF16)
    kvt[0, :, 128:640] = jnp.transpose(kv[0, 128:640])
    kvt[1, :, 128:640] = jnp.transpose(kv[1, 128:640])
    dzt[...] = jnp.transpose(nn(gather, dz_ref[...]).astype(BF16))
    k2m[...] = jnp.where(
        head_lane, nn(kvt[0, :, 128:640], pool2t[...]) * (1.0 / 16), 0.0
    ).astype(BF16)
    v2m[...] = jnp.where(head_lane, nn(kvt[1, :, 128:640], pool2t[...]), 0.0).astype(BF16)

    has_left = jnp.where(me > 0, 0.0, NEG).astype(F32)
    has_right = jnp.where(me < n - 1, 0.0, NEG).astype(F32)
    key_sub = (iota((WIN2, 256), 0) >> 5) - 4
    query_sub = (iota((WIN2, 256), 1) & 127) >> 5
    apart = jnp.where(jnp.abs(key_sub - query_sub) > 1, 0.0, NEG)
    bias1[0:BLK] = apart[0:BLK] + has_left
    bias1[BLK : 2 * BLK] = apart[BLK : 2 * BLK]
    bias1[2 * BLK :] = apart[2 * BLK :] + has_right
    for slot in range(12):
        if slot < SLOTS:
            device = base + 2 * chips[slot // 2] + slot % 2
            valid = (device >= 0) & (device < n) & (jnp.abs(device - me) > 1)
            level = jnp.where(valid, 0.0, NEG).astype(F32)
        else:
            level = jnp.float32(NEG)
        bias2[32 * slot : 32 * slot + 32] = jnp.zeros((32, 256), F32) + level
    for which in range(3):
        kv2[which, 320:384] = jnp.zeros((64, FEAT), BF16)
    g2win[320:384] = jnp.zeros((64, 640), BF16)

    def lanes(pair):
        return pl.ds(pl.multiple_of(BLK * pair, BLK), BLK)

    def forward(pair, pos):
        at = lanes(pair)
        start = WINDOW[pos]
        raw = nn(kv[0, start : start + 384, at], two_heads(qg[0, pos, at, :]))
        pieces = [raw[BLK * i : BLK * (i + 1)] for i in range(3)]
        if pos == POS[0]:
            pieces[0] = pieces[0] + has_left
        if pos == POS[3]:
            pieces[2] = pieces[2] + has_right
        if pos == LEVEL1:
            pieces = [piece + bias1[BLK * i : BLK * (i + 1)] for i, piece in enumerate(pieces)]
        top = jnp.max(jnp.maximum(jnp.maximum(pieces[0], pieces[1]), pieces[2]), axis=0, keepdims=True)
        total = None
        rounded = []
        for i, piece in enumerate(pieces):
            piece = jnp.exp(piece - top)
            weights[pos, pair, BLK * i : BLK * (i + 1)] = piece
            total = piece if total is None else total + piece
            rounded.append(piece.astype(BF16))
        total = jnp.sum(total, axis=0, keepdims=True) * (4.0 if pos == LEVEL1 else 1.0)
        result = nn(kvt[1, at, start : start + 384], jnp.concatenate(rounded, axis=0))
        numer[pos, at, :] = own_blocks(result)
        for e in range(2):
            stats[0, pos, pl.ds(2 * pair + e, 1), :] = top[:, BLK * e : BLK * (e + 1)]
            sums[pos, pl.ds(2 * pair + e, 1), :] = total[:, BLK * e : BLK * (e + 1)]

    def over_pairs(body):
        def step(pair, carry):
            body(pair)
            return carry

        lax.fori_loop(0, 4, step, 0)

    def forward_inner(pair):
        forward(pair, 0)
        forward(pair, 1)

    over_pairs(forward_inner)

    for j in range(5):
        arrival(0, 2 * j + core).wait_recv()
        relay_copy(0, j).start()

    for side in range(2):
        kv0_copy(side).wait_recv()
        kv1_copy(side).wait_recv()
    for which in range(2):
        kvt[which, :, 0:128] = jnp.transpose(kv[which, 0:128])
        kvt[which, :, 640:1152] = jnp.transpose(kv[which, 640:1152])

    def forward_rim(pair):
        forward(pair, 2)
        forward(pair, 3)
        forward(pair, 4)

    over_pairs(forward_rim)

    for j in range(5):
        arrival(0, 2 * j + 1 - core).wait_recv()
    for which in range(2):
        kv2t[which] = jnp.transpose(kv2[which])
    scores = nn(kv2[0], q2m[...]) + bias2[...]
    top2 = jnp.max(scores, axis=0, keepdims=True)
    scores = jnp.exp(scores - top2)
    weights2[...] = scores
    total2 = jnp.sum(scores, axis=0, keepdims=True) * 16.0
    numer2[...] = jnp.where(head_lane, nn(kv2t[1], scores.astype(BF16)), 0.0)

    def by_block(ref):
        return jnp.concatenate([ref[POS[b]] for b in range(4)], axis=1)

    head_row = iota((HEADS, 256), 0) == (iota((HEADS, 256), 1) >> 5)

    def rows2(x):
        return jnp.where(head_row, jnp.broadcast_to(x, (HEADS, 256)), 0.0)

    tops = [
        by_block(stats.at[0]),
        spread(stats[0, LEVEL1], pool1[...], 3),
        spread(rows2(top2), pool2[...], 3),
    ]
    totals = [
        by_block(sums),
        spread(sums[LEVEL1], pool1[...], 3),
        spread(rows2(total2), pool2[...], 3),
    ]
    best = jnp.maximum(jnp.maximum(tops[0], tops[1]), tops[2])
    scales = [jnp.exp(top - best) for top in tops]
    denom = scales[0] * totals[0] + scales[1] * totals[1] + scales[2] * totals[2]
    for level in range(3):
        share[level] = scales[level] / denom

    def combine(pair):
        at = lanes(pair)
        fine = jnp.concatenate([numer[POS[b], at, :] for b in range(4)], axis=1)
        middle = spread(numer[LEVEL1, at, :], pool1[...], 2)
        coarse = spread(numer2[at, :], pool2[...], 2)
        grads = dzt[at, :].astype(F32)
        for e in range(2):
            head = 2 * pair + e
            cut = slice(HEAD_DIM * e, HEAD_DIM * (e + 1))
            to = pl.ds(pl.multiple_of(HEAD_DIM * head, HEAD_DIM), HEAD_DIM)
            parts = [share[level, pl.ds(head, 1), :] for level in range(3)]
            grad = grads[cut]
            value = parts[0] * fine[cut] + parts[1] * middle[cut] + parts[2] * coarse[cut]
            mixed[to, :] = value.astype(BF16)
            delta[pl.ds(head, 1), :] = jnp.sum(grad * value, axis=0, keepdims=True)
            own = (parts[0] * grad).astype(BF16)
            for b in range(4):
                qg[1, POS[b], to, :] = own[:, BLK * b : BLK * (b + 1)]
            qg[1, LEVEL1, to, :] = spread(parts[1] * grad, pool1t[...], 2).astype(BF16)
            pooled = spread(parts[2] * grad, pool2t[...], 2)
            keep = (iota((HEAD_DIM, 256), 1) >> 5) == head
            g2m[to, :] = jnp.where(keep, pooled, 0.0).astype(BF16)

    over_pairs(combine)

    energy = share[0] * delta[...]
    for b in range(4):
        stats[1, POS[b]] = energy[:, BLK * b : BLK * (b + 1)]
    stats[1, LEVEL1] = spread(share[1] * delta[...], pool1t[...], 3) * 4.0
    energy2 = jnp.sum(
        jnp.where(head_row, spread(share[2] * delta[...], pool2t[...], 3), 0.0), axis=0, keepdims=True
    ) * 16.0

    pick = iota((32, 256), 0) == (iota((32, 256), 1) & 31)
    g2own[:, 0:FEAT] = nt(onehot(pick), g2m[...]).astype(BF16)
    packed = None
    for i, part in enumerate(parts_of(top2, 3) + parts_of(energy2, 3)):
        chosen = jnp.where(pick, jnp.broadcast_to(part.astype(F32), (32, 256)), 0.0).astype(BF16)
        target = onehot(iota((256, BLK), 1) == (iota((256, BLK), 0) >> 5) + 8 * i)
        term = nn(chosen, target)
        packed = term if packed is None else packed + term
    g2own[:, FEAT:] = packed.astype(BF16)
    for j in range(5):
        direct_copy(1, j).start()
    for side in range(2):
        qg_copy(side, 1).start()
        stats_copy(side).start()

    def pair_row(ref, pair):
        return jnp.concatenate([ref[pl.ds(2 * pair + e, 1), :] for e in range(2)], axis=1)

    def backward(pair):
        at = lanes(pair)
        key_sum, value_sum = {}, {}
        for pos in range(5):
            start = WINDOW[pos]
            window = slice(start, start + 384)
            query_m = two_heads(qg[0, pos, at, :])
            grad_m = two_heads(qg[1, pos, at, :])
            mixing = nn(kv[1, window, at], grad_m)
            weight = weights[pos, pair]
            diff = (weight * (mixing - pair_row(stats.at[1, pos], pair))).astype(BF16)
            dqt[pos, at, :] = own_blocks(nn(kvt[0, at, window], diff))
            own = [i for i in range(3) if 128 <= start + BLK * i < 640 or start + BLK * i == OWN1]
            rows = slice(BLK * own[0], BLK * (own[-1] + 1))
            key_part = nt(diff[rows], query_m)
            value_part = nt(weight[rows].astype(BF16), grad_m)
            for i in own:
                block = (start + BLK * i - 128) // BLK if pos != LEVEL1 else 4
                cut = slice(BLK * (i - own[0]), BLK * (i - own[0] + 1))
                for held, part in ((key_sum, key_part), (value_sum, value_part)):
                    held[block] = part[cut] if block not in held else held[block] + part[cut]
        for block in range(5):
            dkv[0, BLK * block : BLK * (block + 1), at] = key_sum[block]
            dkv[1, BLK * block : BLK * (block + 1), at] = value_sum[block]

    over_pairs(backward)

    for j in range(5):
        arrival(1, 2 * j + core).wait_recv()
        relay_copy(1, j).start()

    mixing2 = nn(kv2[1], g2m[...])
    diff2 = (weights2[...] * (mixing2 - energy2)).astype(BF16)
    dq2[...] = jnp.where(head_lane, nn(kv2t[0], diff2), 0.0)

    for side in range(2):
        qg_copy(side, 0).wait_recv()
        qg_copy(side, 1).wait_recv()
        stats_copy(side).wait_recv()

    far_query = (iota((BLK, 256), 1) & 127) >> 5
    far_key = iota((BLK, 256), 0) >> 5
    far_bias = [
        jnp.where(jnp.abs(far_key - far_query + 4) > 1, 0.0, NEG) + has_left,
        jnp.where(jnp.abs(far_key - far_query - 4) > 1, 0.0, NEG) + has_right,
    ]
    for side in range(2):
        bias1[BLK * side : BLK * (side + 1)] = far_bias[side]

    def from_halo(pair):
        at = lanes(pair)
        for level in range(2):
            key_sum = []
            for side in range(2):
                which = (1 - level) if side == 0 else level
                row = (128, 512)[side] if level == 0 else OWN1
                query_m = two_heads(halo_qg[side, 0, which, at, :])
                grad_m = two_heads(halo_qg[side, 1, which, at, :])
                score = nn(kv[0, row : row + BLK, at], query_m)
                if level == 0:
                    score = score + (has_left, has_right)[side]
                else:
                    score = score + bias1[BLK * side : BLK * (side + 1)]
                weight = jnp.exp(score - pair_row(halo_stats.at[side, 0, which], pair))
                mixing = nn(kv[1, row : row + BLK, at], grad_m)
                diff = weight * (mixing - pair_row(halo_stats.at[side, 1, which], pair))
                key_part = nt(diff.astype(BF16), query_m)
                value_part = nt(weight.astype(BF16), grad_m)
                to = (row - 128) if level == 0 else 512
                dkv[0, to : to + BLK, at] += key_part
                dkv[1, to : to + BLK, at] += value_part

    over_pairs(from_halo)

    for j in range(5):
        arrival(1, 2 * j + 1 - core).wait_recv()
    far_stats = g2win[:, FEAT:]
    stat_row = iota((BLK, 256), 0)
    same_head = (stat_row & 7) == (iota((BLK, 256), 1) >> 5)
    far_top = nn(far_stats, onehot(same_head & (stat_row < 24)))
    far_energy = nn(far_stats, onehot(same_head & (stat_row >= 24) & (stat_row < 48)))
    far_scores = nn(kv2[2], k2m[...]) + bias2[...]
    far_weight = jnp.exp(far_scores - far_top)
    far_mixing = nn(g2win[:, 0:FEAT], v2m[...])
    far_diff = (far_weight * (far_mixing - far_energy)).astype(BF16)
    lane_head = (iota((256, FEAT), 0) >> 5) == (iota((256, FEAT), 1) >> 6)
    dk2 = jnp.where(lane_head, nn(jnp.transpose(far_diff), kv2[2]), 0.0)
    dv2 = jnp.where(lane_head, nn(jnp.transpose(far_weight.astype(BF16)), g2win[:, 0:FEAT]), 0.0)

    def spread_rows(matrix, x):
        high, low = parts_of(x, 2)
        return nn(matrix, high) + nn(matrix, low)

    out_ref[...] = nt(place[...], mixed[...]).astype(BF16)
    query_grad = jnp.concatenate([dqt[POS[b]] for b in range(4)], axis=1)
    query_grad = query_grad + spread(dqt[LEVEL1] * 0.25, pool1[...], 2)
    query_grad = (query_grad + spread(dq2[...] * (1.0 / 16), pool2[...], 2)) * SCALE
    dq_out[...] = nt(place[...], query_grad.astype(BF16)).astype(BF16)
    key_grad = dkv[0, 0:ROWS] + spread_rows(pool1t[...], dkv[0, ROWS:] * 0.25)
    key_grad = key_grad + spread_rows(pool2t[...], dk2 * (1.0 / 16))
    dk_out[...] = nn(place[...], key_grad.astype(BF16)).astype(BF16)
    value_grad = dkv[1, 0:ROWS] + spread_rows(pool1t[...], dkv[1, ROWS:])
    value_grad = value_grad + spread_rows(pool2t[...], dv2)
    dv_out[...] = nn(place[...], value_grad.astype(BF16)).astype(BF16)

    for side in range(2):
        kv0_copy(side).wait_send()
        kv1_copy(side).wait_send()
        qg_copy(side, 0).wait_send()
        qg_copy(side, 1).wait_send()
        stats_copy(side).wait_send()
    for phase in range(2):
        for j in range(5):
            direct_copy(phase, j).wait_send()
            relay_copy(phase, j).wait_send()


def on_device(n, query_points, key_points, value_points, cotangent, hilbert_order):
    shape = jax.ShapeDtypeStruct((ROWS, FEAT), BF16)
    scratch = [
        ((ROWS, ROWS), BF16),
        ((BLK, ROWS), BF16),
        ((ROWS, BLK), BF16),
        ((256, ROWS), BF16),
        ((ROWS, 256), BF16),
        ((2, 1152, FEAT), BF16),
        ((2, FEAT, 1152), BF16),
        ((3, 32, FEAT), BF16),
        ((3, WIN2, FEAT), BF16),
        ((2, FEAT, WIN2), BF16),
        ((2, 5, FEAT, BLK), BF16),
        ((2, 2, 2, FEAT, BLK), BF16),
        ((2, 5, HEADS, BLK), F32),
        ((2, 2, 2, HEADS, BLK), F32),
        ((FEAT, ROWS), BF16),
        ((5, 4, 384, 256), F32),
        ((5, HEADS, BLK), F32),
        ((5, FEAT, BLK), F32),
        ((FEAT, 256), BF16),
        ((FEAT, 256), BF16),
        ((FEAT, 256), BF16),
        ((FEAT, 256), BF16),
        ((WIN2, 256), F32),
        ((FEAT, 256), F32),
        ((32, 640), BF16),
        ((WIN2, 640), BF16),
        ((WIN2, 256), F32),
        ((WIN2, 256), F32),
        ((3, HEADS, ROWS), F32),
        ((HEADS, ROWS), F32),
        ((FEAT, ROWS), BF16),
        ((5, FEAT, BLK), F32),
        ((FEAT, 256), F32),
        ((2, ROWS + BLK, FEAT), F32),
    ]
    return pl.pallas_call(
        functools.partial(kernel, n),
        out_shape=(shape,) * 4,
        in_specs=[pl.BlockSpec(memory_space=pltpu.VMEM)] * 5,
        out_specs=(pl.BlockSpec(memory_space=pltpu.VMEM),) * 4,
        scratch_shapes=[pltpu.VMEM(dims, kind) for dims, kind in scratch]
        + [
            pltpu.SemaphoreType.DMA((2, 5)),
            pltpu.SemaphoreType.DMA((2, 5)),
            pltpu.SemaphoreType.DMA((2, 10)),
            pltpu.SemaphoreType.DMA((2, SLOTS)),
        ],
        compiler_params=pltpu.CompilerParams(
            collective_id=0, has_side_effects=True, vmem_limit_bytes=60 * 1024 * 1024
        ),
        cost_estimate=pl.CostEstimate(
            flops=8_000_000_000, bytes_accessed=4 * 1024 * 1024, transcendentals=2_500_000
        ),
    )(hilbert_order.reshape(1, ROWS), query_points, key_points, value_points, cotangent)


def solution(mesh):
    return jax.shard_map(
        functools.partial(on_device, mesh.shape["seq"]),
        mesh=mesh,
        in_specs=(P("seq", None),) * 4 + (P("seq"),),
        out_specs=(P("seq", None),) * 4,
        check_vma=False,
    )
```

```python
import functools

import jax
import jax.numpy as jnp
from jax import lax
from jax.experimental import pallas as pl
from jax.experimental.pallas import tpu as pltpu
from jax.sharding import PartitionSpec as P

HEADS = 8
HEAD_DIM = 64
FEAT = 512
BLK = 128
ROWS = 512
SCALE = HEAD_DIM**-0.5
NEG = -1e30
MESH = pl.DeviceIdType.MESH
F32 = jnp.float32
BF16 = jnp.bfloat16

POS = {1: 0, 2: 1, 0: 2, 3: 4}
LEVEL1 = 3
WINDOW = {0: 128, 1: 256, 2: 0, 3: 768, 4: 384}
OWN1 = 768 + BLK
SLOTS = 10
WIN2 = 384


def nn(a, b):
    return lax.dot_general(a, b, (((1,), (0,)), ((), ())), preferred_element_type=F32)


def nt(a, b):
    return lax.dot_general(a, b, (((1,), (1,)), ((), ())), preferred_element_type=F32)


def iota(shape, dim):
    return lax.broadcasted_iota(jnp.int32, shape, dim)


def onehot(mask):
    return jnp.where(mask, 1.0, 0.0).astype(BF16)


def parts_of(x, count):
    parts = []
    for _ in range(count):
        part = x.astype(BF16)
        parts.append(part)
        x = x - part.astype(F32)
    return parts


def spread(x, matrix, count):
    total = None
    for part in parts_of(x, count):
        term = nn(part, matrix)
        total = term if total is None else total + term
    return total


def two_heads(x):
    zero = jnp.zeros((HEAD_DIM, x.shape[1]), x.dtype)
    upper = jnp.concatenate([x[:HEAD_DIM], zero], axis=1)
    lower = jnp.concatenate([zero, x[HEAD_DIM:]], axis=1)
    return jnp.concatenate([upper, lower], axis=0)


def own_blocks(x):
    return jnp.concatenate([x[:HEAD_DIM, :BLK], x[HEAD_DIM:, BLK:]], axis=0)


def kernel(
    n,
    order_ref,
    q_any,
    k_any,
    v_any,
    dz_any,
    out_any,
    inputs,
    outputs,
    pool1,
    pool1t,
    pool2,
    pool2t,
    kv,
    kvt,
    kv2own,
    kv2,
    q2own,
    q2win,
    kv2t,
    qg,
    halo_qg,
    stats,
    halo_stats,
    dzt,
    weights,
    sums,
    numer,
    q2m,
    g2m,
    k2m,
    v2m,
    weights2,
    numer2,
    g2own,
    g2win,
    bias1,
    bias2,
    share,
    delta,
    dqt,
    dkv,
    nb_send,
    nb_recv,
    l2_send,
    l2_recv,
    in_sem,
    out_sem,
):
    me = lax.axis_index("seq")
    left = lax.rem(me + n - 1, n)
    right = lax.rem(me + 1, n)
    core = lax.rem(me, 2)
    half = lax.rem(me // 2, 2)
    base = 4 * (me // 4 - 1)
    sibling = me + 1 - 2 * core
    chips = [0, 1, 3 - half, 4, 5]
    peers = [lax.rem(base + 2 * chip + core + n, n) for chip in chips]
    far_dense = [half + 3, half + 3, 2, half, half]

    has_prev = me >= 4
    has_next = me < n - 4
    reach = [has_prev, has_prev, me >= 0, has_next, has_next]
    near = [me > 0, me < n - 1]

    barrier = pltpu.get_barrier_semaphore()

    def greet(device):
        pl.semaphore_signal(barrier, inc=1, device_id=(device,), device_id_type=MESH)

    for device, there in zip([left, right] + peers, near + reach):
        pl.when(there)(functools.partial(greet, device))
    partners = sum(there.astype(jnp.int32) for there in near + reach)

    def load(i):
        return pltpu.make_async_copy((k_any, v_any, q_any, dz_any)[i], inputs.at[i], in_sem.at[i])

    def store(i):
        return pltpu.make_async_copy(outputs.at[i], out_any.at[i], out_sem.at[i])

    for i in range(4):
        load(i).start()

    def remote(src, dst, send, recv, device):
        return pltpu.make_async_remote_copy(
            src_ref=src,
            dst_ref=dst,
            send_sem=send,
            recv_sem=recv,
            device_id=(device,),
            device_id_type=MESH,
        )

    def kv0_copy(side):
        src, dst, to = [(512, 0, right), (128, 640, left)][side]
        return remote(
            kv.at[:, pl.ds(src, BLK)], kv.at[:, pl.ds(dst, BLK)],
            nb_send.at[side, 0], nb_recv.at[side, 0], to,
        )

    def kv1_copy(side):
        dst, to = [(768, right), (1024, left)][side]
        return remote(
            kv.at[:, pl.ds(OWN1, BLK)], kv.at[:, pl.ds(dst, BLK)],
            nb_send.at[side, 1], nb_recv.at[side, 1], to,
        )

    def qg_copy(side, which):
        src, to = [(3, right), (2, left)][side]
        return remote(
            qg.at[which, pl.ds(src, 2)], halo_qg.at[side, which],
            nb_send.at[side, 2 + which], nb_recv.at[side, 2 + which], to,
        )

    def stats_copy(side):
        src, to = [(3, right), (2, left)][side]
        return remote(
            stats.at[:, pl.ds(src, 2)], halo_stats.at[side],
            nb_send.at[side, 4], nb_recv.at[side, 4], to,
        )

    def slot_rows(slot):
        return pl.ds(pl.multiple_of(32 * slot, 32), 32)

    def far_refs(phase, slot):
        if phase == 0:
            return kv2own, kv2.at[:, slot_rows(slot)]
        if phase == 1:
            return q2own, q2win.at[slot_rows(slot)]
        return g2own, g2win.at[slot_rows(slot)]

    def direct_copy(phase, j):
        slot = 2 * far_dense[j] + core
        src, dst = far_refs(phase, slot)
        return remote(src, dst, l2_send.at[phase, j], l2_recv.at[phase, slot], peers[j])

    def arrival(phase, slot):
        src, dst = far_refs(phase, slot)
        return remote(src, dst, l2_send.at[phase, 0], l2_recv.at[phase, slot], sibling)

    def relay_copy(phase, j):
        slot = 2 * j + core
        _, dst = far_refs(phase, slot)
        return remote(dst, dst, l2_send.at[phase, 5 + j], l2_recv.at[phase, slot], sibling)

    def send(copies):
        for side in range(2):
            pl.when(near[1 - side])(copies(side).start)

    def receive(copies):
        for side in range(2):
            pl.when(near[side])(copies(side).wait_recv)

    def sent(copies):
        for side in range(2):
            pl.when(near[1 - side])(copies(side).wait_send)

    def far_send(phase):
        for j in range(5):
            pl.when(reach[j])(direct_copy(phase, j).start)

    def far_relay(phase):
        for j in range(5):
            def step(j=j):
                arrival(phase, 2 * j + core).wait_recv()
                relay_copy(phase, j).start()

            pl.when(reach[j])(step)

    def far_receive(phase):
        for j in range(5):
            pl.when(reach[j])(arrival(phase, 2 * j + 1 - core).wait_recv)

    def clear(rows):
        for first in rows:
            kv[:, first : first + BLK] = jnp.zeros((2, BLK, FEAT), BF16)

    def clear_side(side):
        clear(((0, 768), (640, 1024))[side])
        halo_qg[side] = jnp.zeros((2, 2, FEAT, BLK), BF16)
        halo_stats[side] = jnp.zeros((2, 2, HEADS, BLK), F32)

    def clear_far(first):
        kv2[:, first : first + 128] = jnp.zeros((2, 128, FEAT), BF16)
        q2win[first : first + 128] = jnp.zeros((128, FEAT), BF16)
        g2win[first : first + 128] = jnp.zeros((128, 640), BF16)

    for side in range(2):
        pl.when(jnp.logical_not(near[side]))(functools.partial(clear_side, side))
    pl.when(jnp.logical_not(has_prev))(functools.partial(clear_far, 0))
    pl.when(jnp.logical_not(has_next))(functools.partial(clear_far, 192))
    kv2[:, 320:384] = jnp.zeros((2, 64, FEAT), BF16)
    q2win[320:384] = jnp.zeros((64, FEAT), BF16)
    g2win[320:384] = jnp.zeros((64, 640), BF16)

    order = order_ref[...] - me * ROWS
    column = jnp.transpose(jnp.broadcast_to(order.astype(F32), (BLK, ROWS)))
    lane = iota((ROWS, BLK), 1).astype(F32)
    gather = jnp.concatenate(
        [jnp.where(column == lane + float(BLK * i), 1.0, 0.0).astype(BF16) for i in range(4)], axis=1
    )
    pool1[...] = onehot(iota((BLK, ROWS), 0) == (iota((BLK, ROWS), 1) >> 2))
    pool1t[...] = onehot((iota((ROWS, BLK), 0) >> 2) == iota((ROWS, BLK), 1))
    pool2[...] = onehot((iota((256, ROWS), 0) & 31) == (iota((256, ROWS), 1) >> 4))
    pool2t[...] = onehot((iota((ROWS, 256), 0) >> 4) == (iota((ROWS, 256), 1) & 31))

    for which in range(2):
        load(which).wait()
        kv[which, 128:640] = nn(gather, inputs[which]).astype(BF16)
    pl.semaphore_wait(barrier, partners)
    send(kv0_copy)
    kv[0, OWN1 : OWN1 + BLK] = (nn(pool1[...], kv[0, 128:640]) * 0.25).astype(BF16)
    kv[1, OWN1 : OWN1 + BLK] = nn(pool1[...], kv[1, 128:640]).astype(BF16)
    send(kv1_copy)
    kv2own[0] = (nn(pool2[0:32], kv[0, 128:640]) * (1.0 / 16)).astype(BF16)
    kv2own[1] = nn(pool2[0:32], kv[1, 128:640]).astype(BF16)
    far_send(0)
    load(2).wait()
    query = (nn(gather, inputs[2]) * SCALE).astype(BF16)
    q2own[...] = (nn(pool2[0:32], query) * (1.0 / 16)).astype(BF16)
    query_t = jnp.transpose(query)
    for b in range(4):
        qg[0, POS[b]] = query_t[:, BLK * b : BLK * (b + 1)]
    qg[0, LEVEL1] = (nn(query_t, pool1t[...]) * 0.25).astype(BF16)

    head_lane = (iota((FEAT, 256), 0) >> 6) == (iota((FEAT, 256), 1) >> 5)
    q2m[...] = jnp.where(head_lane, nn(query_t, pool2t[...]) * (1.0 / 16), 0.0).astype(BF16)
    kvt[0, :, 128:640] = jnp.transpose(kv[0, 128:640])
    kvt[1, :, 128:640] = jnp.transpose(kv[1, 128:640])
    load(3).wait()
    dzt[...] = jnp.transpose(nn(gather, inputs[3]).astype(BF16))
    k2m[...] = jnp.where(
        head_lane, nn(kvt[0, :, 128:640], pool2t[...]) * (1.0 / 16), 0.0
    ).astype(BF16)
    v2m[...] = jnp.where(head_lane, nn(kvt[1, :, 128:640], pool2t[...]), 0.0).astype(BF16)

    has_left = jnp.where(me > 0, 0.0, NEG).astype(F32)
    has_right = jnp.where(me < n - 1, 0.0, NEG).astype(F32)
    key_sub = (iota((WIN2, 256), 0) >> 5) - 4
    query_sub = (iota((WIN2, 256), 1) & 127) >> 5
    apart = jnp.where(jnp.abs(key_sub - query_sub) > 1, 0.0, NEG)
    bias1[0:BLK] = apart[0:BLK] + has_left
    bias1[BLK : 2 * BLK] = apart[BLK : 2 * BLK]
    bias1[2 * BLK :] = apart[2 * BLK :] + has_right
    for slot in range(12):
        if slot < SLOTS:
            device = base + 2 * chips[slot // 2] + slot % 2
            valid = (device >= 0) & (device < n) & (jnp.abs(device - me) > 1)
            level = jnp.where(valid, 0.0, NEG).astype(F32)
        else:
            level = jnp.float32(NEG)
        bias2[32 * slot : 32 * slot + 32] = jnp.zeros((32, 256), F32) + level

    def lanes(pair):
        return pl.ds(pl.multiple_of(BLK * pair, BLK), BLK)

    def forward(pair, pos):
        at = lanes(pair)
        start = WINDOW[pos]
        raw = nn(kv[0, start : start + 384, at], two_heads(qg[0, pos, at, :]))
        pieces = [raw[BLK * i : BLK * (i + 1)] for i in range(3)]
        if pos == POS[0]:
            pieces[0] = pieces[0] + has_left
        if pos == POS[3]:
            pieces[2] = pieces[2] + has_right
        if pos == LEVEL1:
            pieces = [piece + bias1[BLK * i : BLK * (i + 1)] for i, piece in enumerate(pieces)]
        top = jnp.max(jnp.maximum(jnp.maximum(pieces[0], pieces[1]), pieces[2]), axis=0, keepdims=True)
        total = None
        rounded = []
        for i, piece in enumerate(pieces):
            piece = jnp.exp(piece - top)
            weights[pos, pair, BLK * i : BLK * (i + 1)] = piece
            total = piece if total is None else total + piece
            rounded.append(piece.astype(BF16))
        total = jnp.sum(total, axis=0, keepdims=True) * (4.0 if pos == LEVEL1 else 1.0)
        result = nn(kvt[1, at, start : start + 384], jnp.concatenate(rounded, axis=0))
        numer[pos, at, :] = own_blocks(result)
        for e in range(2):
            stats[0, pos, pl.ds(2 * pair + e, 1), :] = top[:, BLK * e : BLK * (e + 1)]
            sums[pos, pl.ds(2 * pair + e, 1), :] = total[:, BLK * e : BLK * (e + 1)]

    def over_pairs(body):
        def step(pair, carry):
            body(pair)
            return carry

        lax.fori_loop(0, 4, step, 0)

    def forward_inner(pair):
        forward(pair, 0)
        forward(pair, 1)

    over_pairs(forward_inner)

    receive(kv0_copy)
    receive(kv1_copy)
    send(lambda side: qg_copy(side, 0))
    far_relay(0)
    far_send(1)
    for which in range(2):
        kvt[which, :, 0:128] = jnp.transpose(kv[which, 0:128])
        kvt[which, :, 640:1152] = jnp.transpose(kv[which, 640:1152])

    def forward_rim(pair):
        forward(pair, 2)
        forward(pair, 3)
        forward(pair, 4)

    over_pairs(forward_rim)

    far_receive(0)
    for which in range(2):
        kv2t[which] = jnp.transpose(kv2[which])
    scores = nn(kv2[0], q2m[...]) + bias2[...]
    top2 = jnp.max(scores, axis=0, keepdims=True)
    scores = jnp.exp(scores - top2)
    weights2[...] = scores
    total2 = jnp.sum(scores, axis=0, keepdims=True) * 16.0
    numer2[...] = jnp.where(head_lane, nn(kv2t[1], scores.astype(BF16)), 0.0)

    def by_block(ref):
        return jnp.concatenate([ref[POS[b]] for b in range(4)], axis=1)

    head_row = iota((HEADS, 256), 0) == (iota((HEADS, 256), 1) >> 5)

    def rows2(x):
        return jnp.where(head_row, jnp.broadcast_to(x, (HEADS, 256)), 0.0)

    tops = [
        by_block(stats.at[0]),
        spread(stats[0, LEVEL1], pool1[...], 3),
        spread(rows2(top2), pool2[...], 3),
    ]
    totals = [
        by_block(sums),
        spread(sums[LEVEL1], pool1[...], 3),
        spread(rows2(total2), pool2[...], 3),
    ]
    best = jnp.maximum(jnp.maximum(tops[0], tops[1]), tops[2])
    scales = [jnp.exp(top - best) for top in tops]
    denom = scales[0] * totals[0] + scales[1] * totals[1] + scales[2] * totals[2]
    for level in range(3):
        share[level] = scales[level] / denom

    def combine(pair):
        at = lanes(pair)
        fine = jnp.concatenate([numer[POS[b], at, :] for b in range(4)], axis=1)
        middle = spread(numer[LEVEL1, at, :], pool1[...], 2)
        coarse = spread(numer2[at, :], pool2[...], 2)
        grads = dzt[at, :].astype(F32)
        for e in range(2):
            head = 2 * pair + e
            cut = slice(HEAD_DIM * e, HEAD_DIM * (e + 1))
            to = pl.ds(pl.multiple_of(HEAD_DIM * head, HEAD_DIM), HEAD_DIM)
            parts = [share[level, pl.ds(head, 1), :] for level in range(3)]
            grad = grads[cut]
            value = parts[0] * fine[cut] + parts[1] * middle[cut] + parts[2] * coarse[cut]
            outputs[0, to, :] = value.astype(BF16)
            delta[pl.ds(head, 1), :] = jnp.sum(grad * value, axis=0, keepdims=True)
            own = (parts[0] * grad).astype(BF16)
            for b in range(4):
                qg[1, POS[b], to, :] = own[:, BLK * b : BLK * (b + 1)]
            qg[1, LEVEL1, to, :] = spread(parts[1] * grad, pool1t[...], 2).astype(BF16)
            pooled = spread(parts[2] * grad, pool2t[...], 2)
            keep = (iota((HEAD_DIM, 256), 1) >> 5) == head
            g2m[to, :] = jnp.where(keep, pooled, 0.0).astype(BF16)

    over_pairs(combine)
    store(0).start()

    energy = share[0] * delta[...]
    for b in range(4):
        stats[1, POS[b]] = energy[:, BLK * b : BLK * (b + 1)]
    stats[1, LEVEL1] = spread(share[1] * delta[...], pool1t[...], 3) * 4.0
    energy2 = jnp.sum(
        jnp.where(head_row, spread(share[2] * delta[...], pool2t[...], 3), 0.0), axis=0, keepdims=True
    ) * 16.0

    pick = iota((32, 256), 0) == (iota((32, 256), 1) & 31)
    g2own[:, 0:FEAT] = nt(onehot(pick), g2m[...]).astype(BF16)
    packed = None
    for i, part in enumerate(parts_of(top2, 3) + parts_of(energy2, 3)):
        chosen = jnp.where(pick, jnp.broadcast_to(part.astype(F32), (32, 256)), 0.0).astype(BF16)
        target = onehot(iota((256, BLK), 1) == (iota((256, BLK), 0) >> 5) + 8 * i)
        term = nn(chosen, target)
        packed = term if packed is None else packed + term
    g2own[:, FEAT:] = packed.astype(BF16)
    send(stats_copy)
    send(lambda side: qg_copy(side, 1))
    far_send(2)

    def pair_row(ref, pair):
        return jnp.concatenate([ref[pl.ds(2 * pair + e, 1), :] for e in range(2)], axis=1)

    def backward(pair):
        at = lanes(pair)
        key_sum, value_sum = {}, {}
        for pos in range(5):
            start = WINDOW[pos]
            window = slice(start, start + 384)
            query_m = two_heads(qg[0, pos, at, :])
            grad_m = two_heads(qg[1, pos, at, :])
            mixing = nn(kv[1, window, at], grad_m)
            weight = weights[pos, pair]
            diff = (weight * (mixing - pair_row(stats.at[1, pos], pair))).astype(BF16)
            dqt[pos, at, :] = own_blocks(nn(kvt[0, at, window], diff))
            own = [i for i in range(3) if 128 <= start + BLK * i < 640 or start + BLK * i == OWN1]
            rows = slice(BLK * own[0], BLK * (own[-1] + 1))
            key_part = nt(diff[rows], query_m)
            value_part = nt(weight[rows].astype(BF16), grad_m)
            for i in own:
                block = (start + BLK * i - 128) // BLK if pos != LEVEL1 else 4
                cut = slice(BLK * (i - own[0]), BLK * (i - own[0] + 1))
                for held, part in ((key_sum, key_part), (value_sum, value_part)):
                    held[block] = part[cut] if block not in held else held[block] + part[cut]
        for block in range(5):
            dkv[0, BLK * block : BLK * (block + 1), at] = key_sum[block]
            dkv[1, BLK * block : BLK * (block + 1), at] = value_sum[block]

    over_pairs(backward)

    far_relay(1)
    far_relay(2)

    mixing2 = nn(kv2[1], g2m[...])
    diff2 = (weights2[...] * (mixing2 - energy2)).astype(BF16)
    dq2 = jnp.where(head_lane, nn(kv2t[0], diff2), 0.0)
    query_grad = jnp.concatenate([dqt[POS[b]] for b in range(4)], axis=1)
    query_grad = query_grad + spread(dqt[LEVEL1] * 0.25, pool1[...], 2)
    query_grad = (query_grad + spread(dq2 * (1.0 / 16), pool2[...], 2)) * SCALE
    outputs[1] = query_grad.astype(BF16)
    store(1).start()

    receive(lambda side: qg_copy(side, 0))
    receive(stats_copy)
    receive(lambda side: qg_copy(side, 1))

    far_query = (iota((BLK, 256), 1) & 127) >> 5
    far_key = iota((BLK, 256), 0) >> 5
    far_bias = [
        jnp.where(jnp.abs(far_key - far_query + 4) > 1, 0.0, NEG) + has_left,
        jnp.where(jnp.abs(far_key - far_query - 4) > 1, 0.0, NEG) + has_right,
    ]
    for side in range(2):
        bias1[BLK * side : BLK * (side + 1)] = far_bias[side]

    def from_halo(pair):
        at = lanes(pair)
        for level in range(2):
            key_sum = []
            for side in range(2):
                which = (1 - level) if side == 0 else level
                row = (128, 512)[side] if level == 0 else OWN1
                query_m = two_heads(halo_qg[side, 0, which, at, :])
                grad_m = two_heads(halo_qg[side, 1, which, at, :])
                score = nn(kv[0, row : row + BLK, at], query_m)
                if level == 0:
                    score = score + (has_left, has_right)[side]
                else:
                    score = score + bias1[BLK * side : BLK * (side + 1)]
                weight = jnp.exp(score - pair_row(halo_stats.at[side, 0, which], pair))
                mixing = nn(kv[1, row : row + BLK, at], grad_m)
                diff = weight * (mixing - pair_row(halo_stats.at[side, 1, which], pair))
                key_part = nt(diff.astype(BF16), query_m)
                value_part = nt(weight.astype(BF16), grad_m)
                to = (row - 128) if level == 0 else 512
                dkv[0, to : to + BLK, at] += key_part
                dkv[1, to : to + BLK, at] += value_part

    over_pairs(from_halo)

    far_receive(1)
    far_receive(2)
    far_stats = g2win[:, FEAT:]
    stat_row = iota((BLK, 256), 0)
    same_head = (stat_row & 7) == (iota((BLK, 256), 1) >> 5)
    far_top = nn(far_stats, onehot(same_head & (stat_row < 24)))
    far_energy = nn(far_stats, onehot(same_head & (stat_row >= 24) & (stat_row < 48)))
    far_scores = nn(q2win[...], k2m[...]) + bias2[...]
    far_weight = jnp.exp(far_scores - far_top)
    far_mixing = nn(g2win[:, 0:FEAT], v2m[...])
    far_diff = (far_weight * (far_mixing - far_energy)).astype(BF16)
    lane_head = (iota((256, FEAT), 0) >> 5) == (iota((256, FEAT), 1) >> 6)
    dk2 = jnp.where(lane_head, nn(jnp.transpose(far_diff), q2win[...]), 0.0)
    dv2 = jnp.where(lane_head, nn(jnp.transpose(far_weight.astype(BF16)), g2win[:, 0:FEAT]), 0.0)

    def spread_rows(matrix, x):
        high, low = parts_of(x, 2)
        return nn(matrix, high) + nn(matrix, low)

    key_grad = dkv[0, 0:ROWS] + spread_rows(pool1t[...], dkv[0, ROWS:] * 0.25)
    key_grad = key_grad + spread_rows(pool2t[...], dk2 * (1.0 / 16))
    outputs[2] = key_grad.astype(BF16)
    store(2).start()
    value_grad = dkv[1, 0:ROWS] + spread_rows(pool1t[...], dkv[1, ROWS:])
    value_grad = value_grad + spread_rows(pool2t[...], dv2)
    outputs[3] = value_grad.astype(BF16)
    store(3).start()

    for copies in (kv0_copy, kv1_copy, lambda side: qg_copy(side, 0), lambda side: qg_copy(side, 1), stats_copy):
        sent(copies)
    for phase in range(3):
        for j in range(5):
            pl.when(reach[j])(direct_copy(phase, j).wait_send)
            pl.when(reach[j])(relay_copy(phase, j).wait_send)
    for i in range(4):
        store(i).wait()


def placing(order_ref, held_any, out_ref, dq_ref, dk_ref, dv_ref, held, results, in_sem, out_sem):
    targets = (out_ref, dq_ref, dk_ref, dv_ref)

    def load(i):
        return pltpu.make_async_copy(held_any.at[i], held.at[i], in_sem.at[i])

    def store(i):
        return pltpu.make_async_copy(results.at[i], targets[i], out_sem.at[i])

    for i in range(4):
        load(i).start()
    order = order_ref[...] - lax.axis_index("seq") * ROWS
    place = onehot(iota((ROWS, ROWS), 0) == order)
    for i in range(4):
        load(i).wait()
        product = nt if i < 2 else nn
        results[i] = product(place, held[i]).astype(BF16)
        store(i).start()
    for i in range(4):
        store(i).wait()


def on_device(n, query_points, key_points, value_points, cotangent, hilbert_order):
    shape = jax.ShapeDtypeStruct((ROWS, FEAT), BF16)
    scratch = [
        ((4, ROWS, FEAT), BF16),
        ((4, ROWS, FEAT), BF16),
        ((BLK, ROWS), BF16),
        ((ROWS, BLK), BF16),
        ((256, ROWS), BF16),
        ((ROWS, 256), BF16),
        ((2, 1152, FEAT), BF16),
        ((2, FEAT, 1152), BF16),
        ((2, 32, FEAT), BF16),
        ((2, WIN2, FEAT), BF16),
        ((32, FEAT), BF16),
        ((WIN2, FEAT), BF16),
        ((2, FEAT, WIN2), BF16),
        ((2, 5, FEAT, BLK), BF16),
        ((2, 2, 2, FEAT, BLK), BF16),
        ((2, 5, HEADS, BLK), F32),
        ((2, 2, 2, HEADS, BLK), F32),
        ((FEAT, ROWS), BF16),
        ((5, 4, 384, 256), F32),
        ((5, HEADS, BLK), F32),
        ((5, FEAT, BLK), F32),
        ((FEAT, 256), BF16),
        ((FEAT, 256), BF16),
        ((FEAT, 256), BF16),
        ((FEAT, 256), BF16),
        ((WIN2, 256), F32),
        ((FEAT, 256), F32),
        ((32, 640), BF16),
        ((WIN2, 640), BF16),
        ((WIN2, 256), F32),
        ((WIN2, 256), F32),
        ((3, HEADS, ROWS), F32),
        ((HEADS, ROWS), F32),
        ((5, FEAT, BLK), F32),
        ((2, ROWS + BLK, FEAT), F32),
    ]
    anywhere = pl.BlockSpec(memory_space=pl.ANY)
    order = hilbert_order.reshape(1, ROWS)
    held = pl.pallas_call(
        functools.partial(kernel, n),
        out_shape=jax.ShapeDtypeStruct((4, ROWS, FEAT), BF16),
        in_specs=[pl.BlockSpec(memory_space=pltpu.VMEM)] + [pl.BlockSpec(memory_space=pltpu.HBM)] * 4,
        out_specs=anywhere,
        scratch_shapes=[pltpu.VMEM(dims, kind) for dims, kind in scratch]
        + [
            pltpu.SemaphoreType.DMA((2, 5)),
            pltpu.SemaphoreType.DMA((2, 5)),
            pltpu.SemaphoreType.DMA((3, 10)),
            pltpu.SemaphoreType.DMA((3, SLOTS)),
            pltpu.SemaphoreType.DMA((4,)),
            pltpu.SemaphoreType.DMA((4,)),
        ],
        compiler_params=pltpu.CompilerParams(
            collective_id=0, has_side_effects=True, vmem_limit_bytes=48 * 1024 * 1024
        ),
        cost_estimate=pl.CostEstimate(
            flops=8_000_000_000, bytes_accessed=4 * 1024 * 1024, transcendentals=2_500_000
        ),
    )(order, *[pltpu.with_memory_space_constraint(x, pltpu.HBM) for x in (query_points, key_points, value_points, cotangent)])
    return pl.pallas_call(
        placing,
        out_shape=(shape,) * 4,
        in_specs=[pl.BlockSpec(memory_space=pltpu.VMEM), anywhere],
        out_specs=(anywhere,) * 4,
        scratch_shapes=[pltpu.VMEM((4, ROWS, FEAT), BF16)] * 2 + [pltpu.SemaphoreType.DMA((4,))] * 2,
        compiler_params=pltpu.CompilerParams(vmem_limit_bytes=16 * 1024 * 1024),
        cost_estimate=pl.CostEstimate(
            flops=1_100_000_000, bytes_accessed=4 * 1024 * 1024, transcendentals=0
        ),
    )(order, held)


def solution(mesh):
    return jax.shard_map(
        functools.partial(on_device, mesh.shape["seq"]),
        mesh=mesh,
        in_specs=(P("seq", None),) * 4 + (P("seq"),),
        out_specs=(P("seq", None),) * 4,
        check_vma=False,
    )
```

```python
import functools

import jax
import jax.numpy as jnp
from jax import lax
from jax.experimental import pallas as pl
from jax.experimental.pallas import tpu as pltpu
from jax.sharding import PartitionSpec as P

HEADS = 8
HEAD_DIM = 64
FEAT = 512
BLK = 128
ROWS = 512
SCALE = HEAD_DIM**-0.5
NEG = -1e30
MESH = pl.DeviceIdType.MESH
F32 = jnp.float32
BF16 = jnp.bfloat16

POS = {1: 0, 2: 1, 0: 2, 3: 4}
LEVEL1 = 3
WINDOW = {0: 128, 1: 256, 2: 0, 3: 768, 4: 384}
OWN1 = 768 + BLK
SLOTS = 10
WIN2 = 384


def nn(a, b):
    return lax.dot_general(a, b, (((1,), (0,)), ((), ())), preferred_element_type=F32)


def nt(a, b):
    return lax.dot_general(a, b, (((1,), (1,)), ((), ())), preferred_element_type=F32)


def iota(shape, dim):
    return lax.broadcasted_iota(jnp.int32, shape, dim)


def onehot(mask):
    return jnp.where(mask, 1.0, 0.0).astype(BF16)


def parts_of(x, count):
    parts = []
    for _ in range(count):
        part = x.astype(BF16)
        parts.append(part)
        x = x - part.astype(F32)
    return parts


def spread(x, matrix, count):
    total = None
    for part in parts_of(x, count):
        term = nn(part, matrix)
        total = term if total is None else total + term
    return total


def two_heads(x):
    zero = jnp.zeros((HEAD_DIM, x.shape[1]), x.dtype)
    upper = jnp.concatenate([x[:HEAD_DIM], zero], axis=1)
    lower = jnp.concatenate([zero, x[HEAD_DIM:]], axis=1)
    return jnp.concatenate([upper, lower], axis=0)


def own_blocks(x):
    return jnp.concatenate([x[:HEAD_DIM, :BLK], x[HEAD_DIM:, BLK:]], axis=0)


def kernel(
    n,
    order_any,
    q_any,
    k_any,
    v_any,
    dz_any,
    out_any,
    order_ref,
    inputs,
    outputs,
    pool1,
    pool1t,
    pool2,
    pool2t,
    kv,
    kvt,
    kv2own,
    kv2,
    q2own,
    q2win,
    kv2t,
    qg,
    halo_qg,
    stats,
    halo_stats,
    dzt,
    weights,
    sums,
    numer,
    q2m,
    g2m,
    k2m,
    v2m,
    weights2,
    numer2,
    g2own,
    g2win,
    bias1,
    bias2,
    share,
    delta,
    dqt,
    dkv,
    nb_send,
    nb_recv,
    l2_send,
    l2_recv,
    in_sem,
    out_sem,
):
    me = lax.axis_index("seq")
    left = lax.rem(me + n - 1, n)
    right = lax.rem(me + 1, n)
    core = lax.rem(me, 2)
    half = lax.rem(me // 2, 2)
    base = 4 * (me // 4 - 1)
    sibling = me + 1 - 2 * core
    chips = [0, 1, 3 - half, 4, 5]
    peers = [lax.rem(base + 2 * chip + core + n, n) for chip in chips]
    far_dense = [half + 3, half + 3, 2, half, half]

    has_prev = me >= 4
    has_next = me < n - 4
    reach = [has_prev, has_prev, me >= 0, has_next, has_next]
    near = [me > 0, me < n - 1]

    barrier = pltpu.get_barrier_semaphore()

    def greet(device):
        pl.semaphore_signal(barrier, inc=1, device_id=(device,), device_id_type=MESH)

    for device, there in zip([left, right] + peers, near + reach):
        pl.when(there)(functools.partial(greet, device))
    partners = sum(there.astype(jnp.int32) for there in near + reach)

    def load(i):
        return pltpu.make_async_copy((k_any, v_any, q_any, dz_any)[i], inputs.at[i], in_sem.at[i])

    def store(i):
        return pltpu.make_async_copy(outputs.at[i], out_any.at[i], out_sem.at[i])

    order_load = pltpu.make_async_copy(order_any, order_ref, in_sem.at[4])
    order_load.start()
    for i in range(4):
        load(i).start()

    def remote(src, dst, send, recv, device):
        return pltpu.make_async_remote_copy(
            src_ref=src,
            dst_ref=dst,
            send_sem=send,
            recv_sem=recv,
            device_id=(device,),
            device_id_type=MESH,
        )

    def kv0_copy(side):
        src, dst, to = [(512, 0, right), (128, 640, left)][side]
        return remote(
            kv.at[:, pl.ds(src, BLK)], kv.at[:, pl.ds(dst, BLK)],
            nb_send.at[side, 0], nb_recv.at[side, 0], to,
        )

    def kv1_copy(side):
        dst, to = [(768, right), (1024, left)][side]
        return remote(
            kv.at[:, pl.ds(OWN1, BLK)], kv.at[:, pl.ds(dst, BLK)],
            nb_send.at[side, 1], nb_recv.at[side, 1], to,
        )

    def qg_copy(side, which):
        src, to = [(3, right), (2, left)][side]
        return remote(
            qg.at[which, pl.ds(src, 2)], halo_qg.at[side, which],
            nb_send.at[side, 2 + which], nb_recv.at[side, 2 + which], to,
        )

    def stats_copy(side):
        src, to = [(3, right), (2, left)][side]
        return remote(
            stats.at[:, pl.ds(src, 2)], halo_stats.at[side],
            nb_send.at[side, 4], nb_recv.at[side, 4], to,
        )

    def slot_rows(slot):
        return pl.ds(pl.multiple_of(32 * slot, 32), 32)

    def far_refs(phase, slot):
        if phase == 0:
            return kv2own, kv2.at[:, slot_rows(slot)]
        if phase == 1:
            return q2own, q2win.at[slot_rows(slot)]
        return g2own, g2win.at[slot_rows(slot)]

    def direct_copy(phase, j):
        slot = 2 * far_dense[j] + core
        src, dst = far_refs(phase, slot)
        return remote(src, dst, l2_send.at[phase, j], l2_recv.at[phase, slot], peers[j])

    def arrival(phase, slot):
        src, dst = far_refs(phase, slot)
        return remote(src, dst, l2_send.at[phase, 0], l2_recv.at[phase, slot], sibling)

    def relay_copy(phase, j):
        slot = 2 * j + core
        _, dst = far_refs(phase, slot)
        return remote(dst, dst, l2_send.at[phase, 5 + j], l2_recv.at[phase, slot], sibling)

    def send(copies):
        for side in range(2):
            pl.when(near[1 - side])(copies(side).start)

    def receive(copies):
        for side in range(2):
            pl.when(near[side])(copies(side).wait_recv)

    def sent(copies):
        for side in range(2):
            pl.when(near[1 - side])(copies(side).wait_send)

    def far_send(phase):
        for j in range(5):
            pl.when(reach[j])(direct_copy(phase, j).start)

    def far_relay(phase):
        for j in range(5):
            def step(j=j):
                arrival(phase, 2 * j + core).wait_recv()
                relay_copy(phase, j).start()

            pl.when(reach[j])(step)

    def far_receive(phase):
        for j in range(5):
            pl.when(reach[j])(arrival(phase, 2 * j + 1 - core).wait_recv)

    def clear(rows):
        for first in rows:
            kv[:, first : first + BLK] = jnp.zeros((2, BLK, FEAT), BF16)

    def clear_side(side):
        clear(((0, 768), (640, 1024))[side])
        halo_qg[side] = jnp.zeros((2, 2, FEAT, BLK), BF16)
        halo_stats[side] = jnp.zeros((2, 2, HEADS, BLK), F32)

    def clear_far(first):
        kv2[:, first : first + 128] = jnp.zeros((2, 128, FEAT), BF16)
        q2win[first : first + 128] = jnp.zeros((128, FEAT), BF16)
        g2win[first : first + 128] = jnp.zeros((128, 640), BF16)

    for side in range(2):
        pl.when(jnp.logical_not(near[side]))(functools.partial(clear_side, side))
    pl.when(jnp.logical_not(has_prev))(functools.partial(clear_far, 0))
    pl.when(jnp.logical_not(has_next))(functools.partial(clear_far, 192))
    kv2[:, 320:384] = jnp.zeros((2, 64, FEAT), BF16)
    q2win[320:384] = jnp.zeros((64, FEAT), BF16)
    g2win[320:384] = jnp.zeros((64, 640), BF16)

    order_load.wait()
    order = order_ref[...] - me * ROWS
    column = jnp.transpose(jnp.broadcast_to(order.astype(F32), (BLK, ROWS)))
    lane = iota((ROWS, BLK), 1).astype(F32)
    gather = jnp.concatenate(
        [jnp.where(column == lane + float(BLK * i), 1.0, 0.0).astype(BF16) for i in range(4)], axis=1
    )
    pool1[...] = onehot(iota((BLK, ROWS), 0) == (iota((BLK, ROWS), 1) >> 2))
    pool1t[...] = onehot((iota((ROWS, BLK), 0) >> 2) == iota((ROWS, BLK), 1))
    pool2[...] = onehot((iota((256, ROWS), 0) & 31) == (iota((256, ROWS), 1) >> 4))
    pool2t[...] = onehot((iota((ROWS, 256), 0) >> 4) == (iota((ROWS, 256), 1) & 31))

    for which in range(2):
        load(which).wait()
        kv[which, 128:640] = nn(gather, inputs[which]).astype(BF16)
    pl.semaphore_wait(barrier, partners)
    send(kv0_copy)
    kv[0, OWN1 : OWN1 + BLK] = (nn(pool1[...], kv[0, 128:640]) * 0.25).astype(BF16)
    kv[1, OWN1 : OWN1 + BLK] = nn(pool1[...], kv[1, 128:640]).astype(BF16)
    send(kv1_copy)
    kv2own[0] = (nn(pool2[0:32], kv[0, 128:640]) * (1.0 / 16)).astype(BF16)
    kv2own[1] = nn(pool2[0:32], kv[1, 128:640]).astype(BF16)
    far_send(0)
    load(2).wait()
    query = (nn(gather, inputs[2]) * SCALE).astype(BF16)
    q2own[...] = (nn(pool2[0:32], query) * (1.0 / 16)).astype(BF16)
    query_t = jnp.transpose(query)
    for b in range(4):
        qg[0, POS[b]] = query_t[:, BLK * b : BLK * (b + 1)]
    qg[0, LEVEL1] = (nn(query_t, pool1t[...]) * 0.25).astype(BF16)

    head_lane = (iota((FEAT, 256), 0) >> 6) == (iota((FEAT, 256), 1) >> 5)
    q2m[...] = jnp.where(head_lane, nn(query_t, pool2t[...]) * (1.0 / 16), 0.0).astype(BF16)
    kvt[0, :, 128:640] = jnp.transpose(kv[0, 128:640])
    kvt[1, :, 128:640] = jnp.transpose(kv[1, 128:640])
    load(3).wait()
    dzt[...] = jnp.transpose(nn(gather, inputs[3]).astype(BF16))
    k2m[...] = jnp.where(
        head_lane, nn(kvt[0, :, 128:640], pool2t[...]) * (1.0 / 16), 0.0
    ).astype(BF16)
    v2m[...] = jnp.where(head_lane, nn(kvt[1, :, 128:640], pool2t[...]), 0.0).astype(BF16)

    has_left = jnp.where(me > 0, 0.0, NEG).astype(F32)
    has_right = jnp.where(me < n - 1, 0.0, NEG).astype(F32)
    key_sub = (iota((WIN2, 256), 0) >> 5) - 4
    query_sub = (iota((WIN2, 256), 1) & 127) >> 5
    apart = jnp.where(jnp.abs(key_sub - query_sub) > 1, 0.0, NEG)
    bias1[0:BLK] = apart[0:BLK] + has_left
    bias1[BLK : 2 * BLK] = apart[BLK : 2 * BLK]
    bias1[2 * BLK :] = apart[2 * BLK :] + has_right
    for slot in range(12):
        if slot < SLOTS:
            device = base + 2 * chips[slot // 2] + slot % 2
            valid = (device >= 0) & (device < n) & (jnp.abs(device - me) > 1)
            level = jnp.where(valid, 0.0, NEG).astype(F32)
        else:
            level = jnp.float32(NEG)
        bias2[32 * slot : 32 * slot + 32] = jnp.zeros((32, 256), F32) + level

    def lanes(pair):
        return slice(BLK * pair, BLK * (pair + 1))

    def head_rows(head):
        return slice(HEAD_DIM * head, HEAD_DIM * (head + 1))

    def forward_scores(pair, pos):
        at = lanes(pair)
        start = WINDOW[pos]
        return nn(kv[0, start : start + 384, at], two_heads(qg[0, pos, at, :]))

    def forward_weights(pair, pos, raw):
        pieces = [raw[BLK * i : BLK * (i + 1)] for i in range(3)]
        if pos == POS[0]:
            pieces[0] = pieces[0] + has_left
        if pos == POS[3]:
            pieces[2] = pieces[2] + has_right
        if pos == LEVEL1:
            pieces = [piece + bias1[BLK * i : BLK * (i + 1)] for i, piece in enumerate(pieces)]
        top = jnp.max(jnp.maximum(jnp.maximum(pieces[0], pieces[1]), pieces[2]), axis=0, keepdims=True)
        total = None
        rounded = []
        for i, piece in enumerate(pieces):
            piece = jnp.exp(piece - top)
            weights[pos, pair, BLK * i : BLK * (i + 1)] = piece
            total = piece if total is None else total + piece
            rounded.append(piece.astype(BF16))
        total = jnp.sum(total, axis=0, keepdims=True) * (4.0 if pos == LEVEL1 else 1.0)
        for e in range(2):
            stats[0, pos, pl.ds(2 * pair + e, 1), :] = top[:, BLK * e : BLK * (e + 1)]
            sums[pos, pl.ds(2 * pair + e, 1), :] = total[:, BLK * e : BLK * (e + 1)]
        return jnp.concatenate(rounded, axis=0)

    def forward_mix(pair, pos, rounded):
        at = lanes(pair)
        start = WINDOW[pos]
        numer[pos, at, :] = own_blocks(nn(kvt[1, at, start : start + 384], rounded))

    def forward_all(units):
        raws = [forward_scores(*unit) for unit in units]
        rounded = [forward_weights(*unit, raw) for unit, raw in zip(units, raws)]
        for unit, value in zip(units, rounded):
            forward_mix(*unit, value)

    def forward_inner(pairs):
        forward_all([(pair, pos) for pair in pairs for pos in (0, 1)])

    forward_inner(range(4))

    receive(kv0_copy)
    receive(kv1_copy)
    send(lambda side: qg_copy(side, 0))
    far_relay(0)
    far_send(1)
    for which in range(2):
        kvt[which, :, 0:128] = jnp.transpose(kv[which, 0:128])
        kvt[which, :, 640:1152] = jnp.transpose(kv[which, 640:1152])

    def forward_rim(pairs):
        forward_all([(pair, pos) for pair in pairs for pos in (2, 4, 3)])

    forward_rim(range(4))

    far_receive(0)
    for which in range(2):
        kv2t[which] = jnp.transpose(kv2[which])
    scores = nn(kv2[0], q2m[...]) + bias2[...]
    top2 = jnp.max(scores, axis=0, keepdims=True)
    scores = jnp.exp(scores - top2)
    weights2[...] = scores
    total2 = jnp.sum(scores, axis=0, keepdims=True) * 16.0
    numer2[...] = jnp.where(head_lane, nn(kv2t[1], scores.astype(BF16)), 0.0)

    def by_block(ref):
        return jnp.concatenate([ref[POS[b]] for b in range(4)], axis=1)

    head_row = iota((HEADS, 256), 0) == (iota((HEADS, 256), 1) >> 5)

    def rows2(x):
        return jnp.where(head_row, jnp.broadcast_to(x, (HEADS, 256)), 0.0)

    tops = [
        by_block(stats.at[0]),
        spread(stats[0, LEVEL1], pool1[...], 3),
        spread(rows2(top2), pool2[...], 3),
    ]
    totals = [
        by_block(sums),
        spread(sums[LEVEL1], pool1[...], 3),
        spread(rows2(total2), pool2[...], 3),
    ]
    best = jnp.maximum(jnp.maximum(tops[0], tops[1]), tops[2])
    scales = [jnp.exp(top - best) for top in tops]
    denom = scales[0] * totals[0] + scales[1] * totals[1] + scales[2] * totals[2]
    for level in range(3):
        share[level] = scales[level] / denom

    def combine(pairs):
        spreads = []
        for pair in pairs:
            at = lanes(pair)
            spreads.append((spread(numer[LEVEL1, at, :], pool1[...], 2), spread(numer2[at, :], pool2[...], 2)))
        scaled = []
        for pair, (middle, coarse) in zip(pairs, spreads):
            at = lanes(pair)
            fine = jnp.concatenate([numer[POS[b], at, :] for b in range(4)], axis=1)
            grads = dzt[at, :].astype(F32)
            for e in range(2):
                head = 2 * pair + e
                cut = slice(HEAD_DIM * e, HEAD_DIM * (e + 1))
                to = head_rows(head)
                parts = [share[level, pl.ds(head, 1), :] for level in range(3)]
                grad = grads[cut]
                value = parts[0] * fine[cut] + parts[1] * middle[cut] + parts[2] * coarse[cut]
                outputs[0, to, :] = value.astype(BF16)
                delta[pl.ds(head, 1), :] = jnp.sum(grad * value, axis=0, keepdims=True)
                own = (parts[0] * grad).astype(BF16)
                for b in range(4):
                    qg[1, POS[b], to, :] = own[:, BLK * b : BLK * (b + 1)]
                scaled.append((head, parts_of(parts[1] * grad, 2), parts_of(parts[2] * grad, 2)))
        for head, middle, coarse in scaled:
            to = head_rows(head)
            qg[1, LEVEL1, to, :] = (nn(middle[0], pool1t[...]) + nn(middle[1], pool1t[...])).astype(BF16)
            pooled = nn(coarse[0], pool2t[...]) + nn(coarse[1], pool2t[...])
            keep = (iota((HEAD_DIM, 256), 1) >> 5) == head
            g2m[to, :] = jnp.where(keep, pooled, 0.0).astype(BF16)

    combine(range(4))
    store(0).start()

    energy = share[0] * delta[...]
    for b in range(4):
        stats[1, POS[b]] = energy[:, BLK * b : BLK * (b + 1)]
    stats[1, LEVEL1] = spread(share[1] * delta[...], pool1t[...], 3) * 4.0
    energy2 = jnp.sum(
        jnp.where(head_row, spread(share[2] * delta[...], pool2t[...], 3), 0.0), axis=0, keepdims=True
    ) * 16.0

    pick = iota((32, 256), 0) == (iota((32, 256), 1) & 31)
    g2own[:, 0:FEAT] = nt(onehot(pick), g2m[...]).astype(BF16)
    packed = None
    for i, part in enumerate(parts_of(top2, 3) + parts_of(energy2, 3)):
        chosen = jnp.where(pick, jnp.broadcast_to(part.astype(F32), (32, 256)), 0.0).astype(BF16)
        target = onehot(iota((256, BLK), 1) == (iota((256, BLK), 0) >> 5) + 8 * i)
        term = nn(chosen, target)
        packed = term if packed is None else packed + term
    g2own[:, FEAT:] = packed.astype(BF16)
    send(stats_copy)
    send(lambda side: qg_copy(side, 1))
    far_send(2)

    def pair_row(ref, pair):
        return jnp.concatenate([ref[pl.ds(2 * pair + e, 1), :] for e in range(2)], axis=1)

    def backward(pairs):
        sums_of = [({}, {}) for pair in pairs]

        def mixing_of(pair, pos):
            at = lanes(pair)
            start = WINDOW[pos]
            return nn(kv[1, start : start + 384, at], two_heads(qg[1, pos, at, :]))

        def diff_of(pair, pos, mixing):
            return (weights[pos, pair] * (mixing - pair_row(stats.at[1, pos], pair))).astype(BF16)

        def grads_of(sums_here, pair, pos, diff):
            at = lanes(pair)
            start = WINDOW[pos]
            query_m = two_heads(qg[0, pos, at, :])
            grad_m = two_heads(qg[1, pos, at, :])
            dqt[pos, at, :] = own_blocks(nn(kvt[0, at, start : start + 384], diff))
            own = [i for i in range(3) if 128 <= start + BLK * i < 640 or start + BLK * i == OWN1]
            rows = slice(BLK * own[0], BLK * (own[-1] + 1))
            key_part = nt(diff[rows], query_m)
            value_part = nt(weights[pos, pair, rows].astype(BF16), grad_m)
            for i in own:
                block = (start + BLK * i - 128) // BLK if pos != LEVEL1 else 4
                cut = slice(BLK * (i - own[0]), BLK * (i - own[0] + 1))
                for held, part in zip(sums_here, (key_part, value_part)):
                    held[block] = part[cut] if block not in held else held[block] + part[cut]
            if pos == 4:
                for which in range(2):
                    for block in range(5):
                        dkv[which, BLK * block : BLK * (block + 1), at] = sums_here[which][block]

        units = [(pair, pos) for pair in pairs for pos in range(5)]
        mixings = [mixing_of(*unit) for unit in units]
        diffs = [diff_of(*unit, mixing) for unit, mixing in zip(units, mixings)]
        for i, (unit, diff) in enumerate(zip(units, diffs)):
            grads_of(sums_of[i // 5], *unit, diff)

    backward(range(4))

    far_relay(1)
    far_relay(2)

    mixing2 = nn(kv2[1], g2m[...])
    diff2 = (weights2[...] * (mixing2 - energy2)).astype(BF16)
    dq2 = jnp.where(head_lane, nn(kv2t[0], diff2), 0.0)
    query_grad = jnp.concatenate([dqt[POS[b]] for b in range(4)], axis=1)
    query_grad = query_grad + spread(dqt[LEVEL1] * 0.25, pool1[...], 2)
    query_grad = (query_grad + spread(dq2 * (1.0 / 16), pool2[...], 2)) * SCALE
    outputs[1] = query_grad.astype(BF16)
    store(1).start()

    receive(lambda side: qg_copy(side, 0))
    receive(stats_copy)
    receive(lambda side: qg_copy(side, 1))

    far_query = (iota((BLK, 256), 1) & 127) >> 5
    far_key = iota((BLK, 256), 0) >> 5
    far_bias = [
        jnp.where(jnp.abs(far_key - far_query + 4) > 1, 0.0, NEG) + has_left,
        jnp.where(jnp.abs(far_key - far_query - 4) > 1, 0.0, NEG) + has_right,
    ]
    for side in range(2):
        bias1[BLK * side : BLK * (side + 1)] = far_bias[side]

    def from_halo(pairs):
        units = [(pair, level, side) for pair in pairs for level in range(2) for side in range(2)]

        def place_of(level, side):
            which = (1 - level) if side == 0 else level
            return which, ((128, 512)[side] if level == 0 else OWN1)

        scores, mixings = [], []
        for pair, level, side in units:
            which, row = place_of(level, side)
            at = lanes(pair)
            scores.append(nn(kv[0, row : row + BLK, at], two_heads(halo_qg[side, 0, which, at, :])))
            mixings.append(nn(kv[1, row : row + BLK, at], two_heads(halo_qg[side, 1, which, at, :])))
        pieces = []
        for (pair, level, side), score, mixing in zip(units, scores, mixings):
            which, row = place_of(level, side)
            if level == 0:
                score = score + (has_left, has_right)[side]
            else:
                score = score + bias1[BLK * side : BLK * (side + 1)]
            weight = jnp.exp(score - pair_row(halo_stats.at[side, 0, which], pair))
            diff = weight * (mixing - pair_row(halo_stats.at[side, 1, which], pair))
            pieces.append((weight.astype(BF16), diff.astype(BF16)))
        parts = []
        for (pair, level, side), (weight, diff) in zip(units, pieces):
            which, row = place_of(level, side)
            at = lanes(pair)
            parts.append(
                (
                    nt(diff, two_heads(halo_qg[side, 0, which, at, :])),
                    nt(weight, two_heads(halo_qg[side, 1, which, at, :])),
                )
            )
        for (pair, level, side), both in zip(units, parts):
            which, row = place_of(level, side)
            at = lanes(pair)
            to = (row - 128) if level == 0 else 512
            for i in range(2):
                dkv[i, to : to + BLK, at] += both[i]

    from_halo(range(4))

    far_receive(1)
    far_receive(2)
    far_stats = g2win[:, FEAT:]
    stat_row = iota((BLK, 256), 0)
    same_head = (stat_row & 7) == (iota((BLK, 256), 1) >> 5)
    far_top = nn(far_stats, onehot(same_head & (stat_row < 24)))
    far_energy = nn(far_stats, onehot(same_head & (stat_row >= 24) & (stat_row < 48)))
    far_scores = nn(q2win[...], k2m[...]) + bias2[...]
    far_weight = jnp.exp(far_scores - far_top)
    far_mixing = nn(g2win[:, 0:FEAT], v2m[...])
    far_diff = (far_weight * (far_mixing - far_energy)).astype(BF16)
    lane_head = (iota((256, FEAT), 0) >> 5) == (iota((256, FEAT), 1) >> 6)
    dk2 = jnp.where(lane_head, nn(jnp.transpose(far_diff), q2win[...]), 0.0)
    dv2 = jnp.where(lane_head, nn(jnp.transpose(far_weight.astype(BF16)), g2win[:, 0:FEAT]), 0.0)

    def spread_rows(matrix, x):
        high, low = parts_of(x, 2)
        return nn(matrix, high) + nn(matrix, low)

    key_grad = dkv[0, 0:ROWS] + spread_rows(pool1t[...], dkv[0, ROWS:] * 0.25)
    key_grad = key_grad + spread_rows(pool2t[...], dk2 * (1.0 / 16))
    outputs[2] = key_grad.astype(BF16)
    store(2).start()
    value_grad = dkv[1, 0:ROWS] + spread_rows(pool1t[...], dkv[1, ROWS:])
    value_grad = value_grad + spread_rows(pool2t[...], dv2)
    outputs[3] = value_grad.astype(BF16)
    store(3).start()

    for copies in (kv0_copy, kv1_copy, lambda side: qg_copy(side, 0), lambda side: qg_copy(side, 1), stats_copy):
        sent(copies)
    for phase in range(3):
        for j in range(5):
            pl.when(reach[j])(direct_copy(phase, j).wait_send)
            pl.when(reach[j])(relay_copy(phase, j).wait_send)
    for i in range(4):
        store(i).wait()


def placing(order_any, held_any, out_ref, dq_ref, dk_ref, dv_ref, order_ref, held, results, in_sem, out_sem):
    targets = (out_ref, dq_ref, dk_ref, dv_ref)

    def load(i):
        return pltpu.make_async_copy(held_any.at[i], held.at[i], in_sem.at[i])

    def store(i):
        return pltpu.make_async_copy(results.at[i], targets[i], out_sem.at[i])

    order_load = pltpu.make_async_copy(order_any, order_ref, in_sem.at[4])
    order_load.start()
    for i in range(4):
        load(i).start()
    order_load.wait()
    order = order_ref[...] - lax.axis_index("seq") * ROWS
    place = onehot(iota((ROWS, ROWS), 0) == order)
    for i in range(4):
        load(i).wait()
        product = nt if i < 2 else nn
        results[i] = product(place, held[i]).astype(BF16)
        store(i).start()
    for i in range(4):
        store(i).wait()


def on_device(n, query_points, key_points, value_points, cotangent, hilbert_order):
    shape = jax.ShapeDtypeStruct((ROWS, FEAT), BF16)
    scratch = [
        ((1, ROWS), jnp.int32),
        ((4, ROWS, FEAT), BF16),
        ((4, ROWS, FEAT), BF16),
        ((BLK, ROWS), BF16),
        ((ROWS, BLK), BF16),
        ((256, ROWS), BF16),
        ((ROWS, 256), BF16),
        ((2, 1152, FEAT), BF16),
        ((2, FEAT, 1152), BF16),
        ((2, 32, FEAT), BF16),
        ((2, WIN2, FEAT), BF16),
        ((32, FEAT), BF16),
        ((WIN2, FEAT), BF16),
        ((2, FEAT, WIN2), BF16),
        ((2, 5, FEAT, BLK), BF16),
        ((2, 2, 2, FEAT, BLK), BF16),
        ((2, 5, HEADS, BLK), F32),
        ((2, 2, 2, HEADS, BLK), F32),
        ((FEAT, ROWS), BF16),
        ((5, 4, 384, 256), F32),
        ((5, HEADS, BLK), F32),
        ((5, FEAT, BLK), F32),
        ((FEAT, 256), BF16),
        ((FEAT, 256), BF16),
        ((FEAT, 256), BF16),
        ((FEAT, 256), BF16),
        ((WIN2, 256), F32),
        ((FEAT, 256), F32),
        ((32, 640), BF16),
        ((WIN2, 640), BF16),
        ((WIN2, 256), F32),
        ((WIN2, 256), F32),
        ((3, HEADS, ROWS), F32),
        ((HEADS, ROWS), F32),
        ((5, FEAT, BLK), F32),
        ((2, ROWS + BLK, FEAT), F32),
    ]
    anywhere = pl.BlockSpec(memory_space=pl.ANY)
    order = hilbert_order.reshape(1, ROWS)
    held = pl.pallas_call(
        functools.partial(kernel, n),
        out_shape=jax.ShapeDtypeStruct((4, ROWS, FEAT), BF16),
        in_specs=[pl.BlockSpec(memory_space=pltpu.HBM)] * 5,
        out_specs=anywhere,
        scratch_shapes=[pltpu.VMEM(dims, kind) for dims, kind in scratch]
        + [
            pltpu.SemaphoreType.DMA((2, 5)),
            pltpu.SemaphoreType.DMA((2, 5)),
            pltpu.SemaphoreType.DMA((3, 10)),
            pltpu.SemaphoreType.DMA((3, SLOTS)),
            pltpu.SemaphoreType.DMA((5,)),
            pltpu.SemaphoreType.DMA((4,)),
        ],
        compiler_params=pltpu.CompilerParams(
            collective_id=0, has_side_effects=True, vmem_limit_bytes=48 * 1024 * 1024
        ),
        cost_estimate=pl.CostEstimate(
            flops=8_000_000_000, bytes_accessed=4 * 1024 * 1024, transcendentals=2_500_000
        ),
    )(
        *[
            pltpu.with_memory_space_constraint(x, pltpu.HBM)
            for x in (order, query_points, key_points, value_points, cotangent)
        ]
    )
    return pl.pallas_call(
        placing,
        out_shape=(shape,) * 4,
        in_specs=[pl.BlockSpec(memory_space=pltpu.HBM), anywhere],
        out_specs=(anywhere,) * 4,
        scratch_shapes=[pltpu.VMEM((1, ROWS), jnp.int32)]
        + [pltpu.VMEM((4, ROWS, FEAT), BF16)] * 2
        + [pltpu.SemaphoreType.DMA((5,)), pltpu.SemaphoreType.DMA((4,))],
        compiler_params=pltpu.CompilerParams(vmem_limit_bytes=16 * 1024 * 1024),
        cost_estimate=pl.CostEstimate(
            flops=1_100_000_000, bytes_accessed=4 * 1024 * 1024, transcendentals=0
        ),
    )(pltpu.with_memory_space_constraint(order, pltpu.HBM), held)


def solution(mesh):
    return jax.shard_map(
        functools.partial(on_device, mesh.shape["seq"]),
        mesh=mesh,
        in_specs=(P("seq", None),) * 4 + (P("seq"),),
        out_specs=(P("seq", None),) * 4,
        check_vma=False,
    )
```

```python
import functools

import jax
import jax.numpy as jnp
from jax import lax
from jax.experimental import pallas as pl
from jax.experimental.pallas import tpu as pltpu
from jax.sharding import PartitionSpec as P

HEADS = 8
HEAD_DIM = 64
FEAT = 512
BLK = 128
ROWS = 512
SCALE = HEAD_DIM**-0.5
NEG = -1e30
MESH = pl.DeviceIdType.MESH
F32 = jnp.float32
BF16 = jnp.bfloat16

POS = {1: 0, 2: 1, 0: 2, 3: 4}
LEVEL1 = 3
WINDOW = {0: 128, 1: 256, 2: 0, 3: 768, 4: 384}
OWN1 = 768 + BLK
SLOTS = 10
WIN2 = 384


def nn(a, b):
    return lax.dot_general(a, b, (((1,), (0,)), ((), ())), preferred_element_type=F32)


def nt(a, b):
    return lax.dot_general(a, b, (((1,), (1,)), ((), ())), preferred_element_type=F32)


def iota(shape, dim):
    return lax.broadcasted_iota(jnp.int32, shape, dim)


def onehot(mask):
    return jnp.where(mask, 1.0, 0.0).astype(BF16)


def parts_of(x, count):
    parts = []
    for _ in range(count):
        part = x.astype(BF16)
        parts.append(part)
        x = x - part.astype(F32)
    return parts


def spread(x, matrix, count):
    total = None
    for part in parts_of(x, count):
        term = nn(part, matrix)
        total = term if total is None else total + term
    return total


def two_heads(x):
    zero = jnp.zeros((HEAD_DIM, x.shape[1]), x.dtype)
    upper = jnp.concatenate([x[:HEAD_DIM], zero], axis=1)
    lower = jnp.concatenate([zero, x[HEAD_DIM:]], axis=1)
    return jnp.concatenate([upper, lower], axis=0)


def own_blocks(x):
    return jnp.concatenate([x[:HEAD_DIM, :BLK], x[HEAD_DIM:, BLK:]], axis=0)


def kernel(
    n,
    order_any,
    q_any,
    k_any,
    v_any,
    dz_any,
    out_any,
    order_ref,
    inputs,
    outputs,
    pool1,
    pool1t,
    pool2,
    pool2t,
    kv,
    kvt,
    kv2own,
    kv2,
    q2own,
    q2win,
    kv2t,
    qg,
    halo_qg,
    stats,
    halo_stats,
    dzt,
    weights,
    sums,
    numer,
    q2m,
    g2m,
    k2m,
    v2m,
    weights2,
    numer2,
    g2own,
    g2win,
    bias1,
    bias2,
    share,
    delta,
    dqt,
    dkv,
    nb_send,
    nb_recv,
    l2_send,
    l2_recv,
    in_sem,
    out_sem,
):
    me = lax.axis_index("seq")
    left = lax.rem(me + n - 1, n)
    right = lax.rem(me + 1, n)
    core = lax.rem(me, 2)
    half = lax.rem(me // 2, 2)
    odd = lax.rem(me // 4, 2)
    base = 4 * (me // 4 - 1)
    sibling = me + 1 - 2 * core
    chips = [0, 1, 3 - half, 4, 5]
    inline = [2, 3 - 3 * odd, 4 - 3 * odd]
    across = [3 * odd, 1 + 3 * odd]
    peers = [base + 2 * chip + core for chip in (3 - half, 4 - 4 * odd, 5 - 4 * odd)]
    row_to = me + 8 - 16 * odd
    row_from = me - 8 + 16 * odd
    to_row = (row_to >= 0) & (row_to < n)
    from_row = (row_from >= 0) & (row_from < n)
    near = [me > 0, me < n - 1]

    barrier = pltpu.get_barrier_semaphore()

    def greet(device):
        pl.semaphore_signal(barrier, inc=1, device_id=(device,), device_id_type=MESH)

    for device in peers:
        greet(device)
    for device, there in ((left, near[0]), (right, near[1]), (row_to, to_row), (row_from, from_row)):
        pl.when(there)(functools.partial(greet, device))
    partners = 3 + sum(there.astype(jnp.int32) for there in near + [to_row, from_row])

    def load(i):
        return pltpu.make_async_copy((k_any, v_any, q_any, dz_any)[i], inputs.at[i], in_sem.at[i])

    def store(i):
        return pltpu.make_async_copy(outputs.at[i], out_any.at[i], out_sem.at[i])

    order_load = pltpu.make_async_copy(order_any, order_ref, in_sem.at[4])
    order_load.start()
    for i in range(4):
        load(i).start()

    def remote(src, dst, send, recv, device):
        return pltpu.make_async_remote_copy(
            src_ref=src,
            dst_ref=dst,
            send_sem=send,
            recv_sem=recv,
            device_id=(device,),
            device_id_type=MESH,
        )

    def kv0_copy(side):
        src, dst, to = [(512, 0, right), (128, 640, left)][side]
        return remote(
            kv.at[:, pl.ds(src, BLK)], kv.at[:, pl.ds(dst, BLK)],
            nb_send.at[side, 0], nb_recv.at[side, 0], to,
        )

    def kv1_copy(side):
        src, dst, to = [(OWN1, 768, right), (OWN1 + 32, 1056, left)][side]
        return remote(
            kv.at[:, pl.ds(src, 96)], kv.at[:, pl.ds(dst, 96)],
            nb_send.at[side, 1], nb_recv.at[side, 1], to,
        )

    def qg_copy(side, which):
        src, to = [(3, right), (2, left)][side]
        return remote(
            qg.at[which, pl.ds(src, 2)], halo_qg.at[side, which],
            nb_send.at[side, 2 + which], nb_recv.at[side, 2 + which], to,
        )

    def stats_copy(side):
        src, to = [(3, right), (2, left)][side]
        return remote(
            stats.at[:, pl.ds(src, 2)], halo_stats.at[side],
            nb_send.at[side, 4], nb_recv.at[side, 4], to,
        )

    def slot_rows(slot):
        return pl.ds(pl.multiple_of(32 * slot, 32), 32)

    def far_refs(phase, slot):
        if phase == 0:
            return kv2own, kv2.at[:, slot_rows(slot)]
        if phase == 1:
            return q2own, q2win.at[slot_rows(slot)]
        return g2own, g2win.at[slot_rows(slot)]

    def direct_copy(phase, i):
        slot = 2 * (2 if i == 0 else half + 3 * odd) + core
        src, dst = far_refs(phase, slot)
        return remote(src, dst, l2_send.at[phase, i], l2_recv.at[phase, slot], peers[i])

    def row_copy(phase, i):
        slot = 2 * across[i] + core
        _, src = far_refs(phase, 2 * inline[1 + i] + core)
        _, dst = far_refs(phase, slot)
        return remote(src, dst, l2_send.at[phase, 3 + i], l2_recv.at[phase, slot], row_to)

    def arrival(phase, slot):
        src, dst = far_refs(phase, slot)
        return remote(src, dst, l2_send.at[phase, 0], l2_recv.at[phase, slot], sibling)

    def relay_copy(phase, i):
        slot = 2 * (inline + across)[i] + core
        _, dst = far_refs(phase, slot)
        return remote(dst, dst, l2_send.at[phase, 5 + i], l2_recv.at[phase, slot], sibling)

    def send(copies):
        for side in range(2):
            pl.when(near[1 - side])(copies(side).start)

    def receive(copies):
        for side in range(2):
            pl.when(near[side])(copies(side).wait_recv)

    def sent(copies):
        for side in range(2):
            pl.when(near[1 - side])(copies(side).wait_send)

    def far_send(phase):
        for i in range(3):
            direct_copy(phase, i).start()

    def far_relay(phase):
        for i in (1, 2, 0):
            arrival(phase, 2 * inline[i] + core).wait_recv()
            if i:
                pl.when(to_row)(row_copy(phase, i - 1).start)
            relay_copy(phase, i).start()

    def far_relay_across(phase):
        for i in range(2):
            def step(i=i):
                arrival(phase, 2 * across[i] + core).wait_recv()
                relay_copy(phase, 3 + i).start()

            pl.when(from_row)(step)

    def far_receive(phase):
        for i in range(3):
            arrival(phase, 2 * inline[i] + 1 - core).wait_recv()
        for i in range(2):
            pl.when(from_row)(arrival(phase, 2 * across[i] + 1 - core).wait_recv)

    def far_sent(phase):
        for i in range(3):
            direct_copy(phase, i).wait_send()
            relay_copy(phase, i).wait_send()
        for i in range(2):
            pl.when(to_row)(row_copy(phase, i).wait_send)
            pl.when(from_row)(relay_copy(phase, 3 + i).wait_send)

    def clear(rows):
        for first in rows:
            kv[:, first : first + BLK] = jnp.zeros((2, BLK, FEAT), BF16)

    def clear_side(side):
        clear(((0, 768), (640, 1024))[side])
        halo_qg[side] = jnp.zeros((2, 2, FEAT, BLK), BF16)
        halo_stats[side] = jnp.zeros((2, 2, HEADS, BLK), F32)

    def clear_far(first):
        kv2[:, first : first + 128] = jnp.zeros((2, 128, FEAT), BF16)
        q2win[first : first + 128] = jnp.zeros((128, FEAT), BF16)
        g2win[first : first + 128] = jnp.zeros((128, 640), BF16)

    order_load.wait()
    order = order_ref[...] - me * ROWS
    column = jnp.transpose(jnp.broadcast_to(order.astype(F32), (BLK, ROWS)))
    lane = iota((ROWS, BLK), 1).astype(F32)
    gather = jnp.concatenate(
        [jnp.where(column == lane + float(BLK * i), 1.0, 0.0).astype(BF16) for i in range(4)], axis=1
    )

    pool2[...] = onehot((iota((256, ROWS), 0) & 31) == (iota((256, ROWS), 1) >> 4))

    for which in range(2):
        load(which).wait()
        kv[which, 128:640] = nn(gather, inputs[which]).astype(BF16)
    kv2own[0] = (nn(pool2[0:32], kv[0, 128:640]) * (1.0 / 16)).astype(BF16)
    kv2own[1] = nn(pool2[0:32], kv[1, 128:640]).astype(BF16)
    pl.semaphore_wait(barrier, partners)
    far_send(0)
    send(kv0_copy)
    pool1[...] = onehot(iota((BLK, ROWS), 0) == (iota((BLK, ROWS), 1) >> 2))
    kv[0, OWN1 : OWN1 + BLK] = (nn(pool1[...], kv[0, 128:640]) * 0.25).astype(BF16)
    kv[1, OWN1 : OWN1 + BLK] = nn(pool1[...], kv[1, 128:640]).astype(BF16)
    send(kv1_copy)
    pool1t[...] = onehot((iota((ROWS, BLK), 0) >> 2) == iota((ROWS, BLK), 1))
    pool2t[...] = onehot((iota((ROWS, 256), 0) >> 4) == (iota((ROWS, 256), 1) & 31))

    for side in range(2):
        pl.when(jnp.logical_not(near[side]))(functools.partial(clear_side, side))
    pl.when(me < 4)(functools.partial(clear_far, 0))
    pl.when(me >= n - 4)(functools.partial(clear_far, 192))
    kv2[:, 320:384] = jnp.zeros((2, 64, FEAT), BF16)
    q2win[320:384] = jnp.zeros((64, FEAT), BF16)
    g2win[320:384] = jnp.zeros((64, 640), BF16)

    load(2).wait()
    query = (nn(gather, inputs[2]) * SCALE).astype(BF16)
    q2own[...] = (nn(pool2[0:32], query) * (1.0 / 16)).astype(BF16)
    query_t = jnp.transpose(query)
    for b in range(4):
        qg[0, POS[b]] = query_t[:, BLK * b : BLK * (b + 1)]
    qg[0, LEVEL1] = (nn(query_t, pool1t[...]) * 0.25).astype(BF16)

    head_lane = (iota((FEAT, 256), 0) >> 6) == (iota((FEAT, 256), 1) >> 5)
    q2m[...] = jnp.where(head_lane, nn(query_t, pool2t[...]) * (1.0 / 16), 0.0).astype(BF16)
    kvt[0, :, 128:640] = jnp.transpose(kv[0, 128:640])
    kvt[1, :, 128:640] = jnp.transpose(kv[1, 128:640])
    load(3).wait()
    dzt[...] = jnp.transpose(nn(gather, inputs[3]).astype(BF16))
    k2m[...] = jnp.where(
        head_lane, nn(kvt[0, :, 128:640], pool2t[...]) * (1.0 / 16), 0.0
    ).astype(BF16)
    v2m[...] = jnp.where(head_lane, nn(kvt[1, :, 128:640], pool2t[...]), 0.0).astype(BF16)

    has_left = jnp.where(me > 0, 0.0, NEG).astype(F32)
    has_right = jnp.where(me < n - 1, 0.0, NEG).astype(F32)
    key_sub = (iota((WIN2, 256), 0) >> 5) - 4
    query_sub = (iota((WIN2, 256), 1) & 127) >> 5
    apart = jnp.where(jnp.abs(key_sub - query_sub) > 1, 0.0, NEG)
    bias1[0:BLK] = apart[0:BLK] + has_left
    bias1[BLK : 2 * BLK] = apart[BLK : 2 * BLK]
    bias1[2 * BLK :] = apart[2 * BLK :] + has_right
    for slot in range(12):
        if slot < SLOTS:
            device = base + 2 * chips[slot // 2] + slot % 2
            valid = (device >= 0) & (device < n) & (jnp.abs(device - me) > 1)
            level = jnp.where(valid, 0.0, NEG).astype(F32)
        else:
            level = jnp.float32(NEG)
        bias2[32 * slot : 32 * slot + 32] = jnp.zeros((32, 256), F32) + level

    def lanes(pair):
        return slice(BLK * pair, BLK * (pair + 1))

    def head_rows(head):
        return slice(HEAD_DIM * head, HEAD_DIM * (head + 1))

    def forward_scores(pair, pos):
        at = lanes(pair)
        start = WINDOW[pos]
        return nn(kv[0, start : start + 384, at], two_heads(qg[0, pos, at, :]))

    def forward_weights(pair, pos, raw):
        pieces = [raw[BLK * i : BLK * (i + 1)] for i in range(3)]
        if pos == POS[0]:
            pieces[0] = pieces[0] + has_left
        if pos == POS[3]:
            pieces[2] = pieces[2] + has_right
        if pos == LEVEL1:
            pieces = [piece + bias1[BLK * i : BLK * (i + 1)] for i, piece in enumerate(pieces)]
        top = jnp.max(jnp.maximum(jnp.maximum(pieces[0], pieces[1]), pieces[2]), axis=0, keepdims=True)
        total = None
        rounded = []
        for i, piece in enumerate(pieces):
            piece = jnp.exp(piece - top)
            weights[pos, pair, BLK * i : BLK * (i + 1)] = piece
            total = piece if total is None else total + piece
            rounded.append(piece.astype(BF16))
        total = jnp.sum(total, axis=0, keepdims=True) * (4.0 if pos == LEVEL1 else 1.0)
        for e in range(2):
            stats[0, pos, pl.ds(2 * pair + e, 1), :] = top[:, BLK * e : BLK * (e + 1)]
            sums[pos, pl.ds(2 * pair + e, 1), :] = total[:, BLK * e : BLK * (e + 1)]
        return jnp.concatenate(rounded, axis=0)

    def forward_mix(pair, pos, rounded):
        at = lanes(pair)
        start = WINDOW[pos]
        numer[pos, at, :] = own_blocks(nn(kvt[1, at, start : start + 384], rounded))

    def forward_all(units):
        raws = [forward_scores(*unit) for unit in units]
        rounded = [forward_weights(*unit, raw) for unit, raw in zip(units, raws)]
        for unit, value in zip(units, rounded):
            forward_mix(*unit, value)

    def forward_inner(pairs):
        forward_all([(pair, pos) for pair in pairs for pos in (0, 1)])

    forward_inner(range(4))

    far_relay(0)
    receive(kv0_copy)
    for which in range(2):
        scale = 0.25 if which == 0 else 1.0
        for source, target in ((0, 864), (640, 1024)):
            pooled = nn(pool1[0:32, 0:BLK], kv[which, source : source + BLK])
            kv[which, target : target + 32] = (pooled * scale).astype(BF16)
    receive(kv1_copy)
    send(lambda side: qg_copy(side, 0))
    far_send(1)
    far_relay_across(0)
    for which in range(2):
        kvt[which, :, 0:128] = jnp.transpose(kv[which, 0:128])
        kvt[which, :, 640:1152] = jnp.transpose(kv[which, 640:1152])

    def forward_rim(pairs):
        forward_all([(pair, pos) for pair in pairs for pos in (2, 4, 3)])

    forward_rim(range(4))

    far_receive(0)
    for which in range(2):
        kv2t[which] = jnp.transpose(kv2[which])
    scores = nn(kv2[0], q2m[...]) + bias2[...]
    top2 = jnp.max(scores, axis=0, keepdims=True)
    scores = jnp.exp(scores - top2)
    weights2[...] = scores
    total2 = jnp.sum(scores, axis=0, keepdims=True) * 16.0
    numer2[...] = jnp.where(head_lane, nn(kv2t[1], scores.astype(BF16)), 0.0)

    def by_block(ref):
        return jnp.concatenate([ref[POS[b]] for b in range(4)], axis=1)

    head_row = iota((HEADS, 256), 0) == (iota((HEADS, 256), 1) >> 5)

    def rows2(x):
        return jnp.where(head_row, jnp.broadcast_to(x, (HEADS, 256)), 0.0)

    tops = [
        by_block(stats.at[0]),
        spread(stats[0, LEVEL1], pool1[...], 3),
        spread(rows2(top2), pool2[...], 3),
    ]
    totals = [
        by_block(sums),
        spread(sums[LEVEL1], pool1[...], 3),
        spread(rows2(total2), pool2[...], 3),
    ]
    best = jnp.maximum(jnp.maximum(tops[0], tops[1]), tops[2])
    scales = [jnp.exp(top - best) for top in tops]
    denom = scales[0] * totals[0] + scales[1] * totals[1] + scales[2] * totals[2]
    for level in range(3):
        share[level] = scales[level] / denom

    def combine(pairs):
        spreads = []
        for pair in pairs:
            at = lanes(pair)
            spreads.append((spread(numer[LEVEL1, at, :], pool1[...], 2), spread(numer2[at, :], pool2[...], 2)))
        scaled = []
        for pair, (middle, coarse) in zip(pairs, spreads):
            at = lanes(pair)
            fine = jnp.concatenate([numer[POS[b], at, :] for b in range(4)], axis=1)
            grads = dzt[at, :].astype(F32)
            for e in range(2):
                head = 2 * pair + e
                cut = slice(HEAD_DIM * e, HEAD_DIM * (e + 1))
                to = head_rows(head)
                parts = [share[level, pl.ds(head, 1), :] for level in range(3)]
                grad = grads[cut]
                value = parts[0] * fine[cut] + parts[1] * middle[cut] + parts[2] * coarse[cut]
                outputs[0, to, :] = value.astype(BF16)
                delta[pl.ds(head, 1), :] = jnp.sum(grad * value, axis=0, keepdims=True)
                own = (parts[0] * grad).astype(BF16)
                for b in range(4):
                    qg[1, POS[b], to, :] = own[:, BLK * b : BLK * (b + 1)]
                scaled.append((head, parts_of(parts[1] * grad, 2), parts_of(parts[2] * grad, 2)))
        for head, middle, coarse in scaled:
            to = head_rows(head)
            qg[1, LEVEL1, to, :] = (nn(middle[0], pool1t[...]) + nn(middle[1], pool1t[...])).astype(BF16)
            pooled = nn(coarse[0], pool2t[...]) + nn(coarse[1], pool2t[...])
            keep = (iota((HEAD_DIM, 256), 1) >> 5) == head
            g2m[to, :] = jnp.where(keep, pooled, 0.0).astype(BF16)

    combine(range(4))
    store(0).start()

    energy = share[0] * delta[...]
    for b in range(4):
        stats[1, POS[b]] = energy[:, BLK * b : BLK * (b + 1)]
    stats[1, LEVEL1] = spread(share[1] * delta[...], pool1t[...], 3) * 4.0
    energy2 = jnp.sum(
        jnp.where(head_row, spread(share[2] * delta[...], pool2t[...], 3), 0.0), axis=0, keepdims=True
    ) * 16.0

    pick = iota((32, 256), 0) == (iota((32, 256), 1) & 31)
    g2own[:, 0:FEAT] = nt(onehot(pick), g2m[...]).astype(BF16)
    packed = None
    for i, part in enumerate(parts_of(top2, 3) + parts_of(energy2, 3)):
        chosen = jnp.where(pick, jnp.broadcast_to(part.astype(F32), (32, 256)), 0.0).astype(BF16)
        target = onehot(iota((256, BLK), 1) == (iota((256, BLK), 0) >> 5) + 8 * i)
        term = nn(chosen, target)
        packed = term if packed is None else packed + term
    g2own[:, FEAT:] = packed.astype(BF16)
    far_send(2)
    send(stats_copy)
    send(lambda side: qg_copy(side, 1))
    far_relay(1)

    def pair_row(ref, pair):
        return jnp.concatenate([ref[pl.ds(2 * pair + e, 1), :] for e in range(2)], axis=1)

    def backward(pairs):
        sums_of = [({}, {}) for pair in pairs]

        def mixing_of(pair, pos):
            at = lanes(pair)
            start = WINDOW[pos]
            return nn(kv[1, start : start + 384, at], two_heads(qg[1, pos, at, :]))

        def diff_of(pair, pos, mixing):
            return (weights[pos, pair] * (mixing - pair_row(stats.at[1, pos], pair))).astype(BF16)

        def grads_of(sums_here, pair, pos, diff):
            at = lanes(pair)
            start = WINDOW[pos]
            query_m = two_heads(qg[0, pos, at, :])
            grad_m = two_heads(qg[1, pos, at, :])
            dqt[pos, at, :] = own_blocks(nn(kvt[0, at, start : start + 384], diff))
            own = [i for i in range(3) if 128 <= start + BLK * i < 640 or start + BLK * i == OWN1]
            rows = slice(BLK * own[0], BLK * (own[-1] + 1))
            key_part = nt(diff[rows], query_m)
            value_part = nt(weights[pos, pair, rows].astype(BF16), grad_m)
            for i in own:
                block = (start + BLK * i - 128) // BLK if pos != LEVEL1 else 4
                cut = slice(BLK * (i - own[0]), BLK * (i - own[0] + 1))
                for held, part in zip(sums_here, (key_part, value_part)):
                    held[block] = part[cut] if block not in held else held[block] + part[cut]
            if pos == 4:
                for which in range(2):
                    for block in range(5):
                        dkv[which, BLK * block : BLK * (block + 1), at] = sums_here[which][block]

        units = [(pair, pos) for pair in pairs for pos in range(5)]
        mixings = [mixing_of(*unit) for unit in units]
        diffs = [diff_of(*unit, mixing) for unit, mixing in zip(units, mixings)]
        for i, (unit, diff) in enumerate(zip(units, diffs)):
            grads_of(sums_of[i // 5], *unit, diff)

    backward(range(4))
    far_relay(2)
    far_relay_across(1)

    mixing2 = nn(kv2[1], g2m[...])
    diff2 = (weights2[...] * (mixing2 - energy2)).astype(BF16)
    dq2 = jnp.where(head_lane, nn(kv2t[0], diff2), 0.0)
    query_grad = jnp.concatenate([dqt[POS[b]] for b in range(4)], axis=1)
    query_grad = query_grad + spread(dqt[LEVEL1] * 0.25, pool1[...], 2)
    query_grad = (query_grad + spread(dq2 * (1.0 / 16), pool2[...], 2)) * SCALE
    outputs[1] = query_grad.astype(BF16)
    store(1).start()

    receive(lambda side: qg_copy(side, 0))
    receive(stats_copy)
    receive(lambda side: qg_copy(side, 1))

    far_query = (iota((BLK, 256), 1) & 127) >> 5
    far_key = iota((BLK, 256), 0) >> 5
    far_bias = [
        jnp.where(jnp.abs(far_key - far_query + 4) > 1, 0.0, NEG) + has_left,
        jnp.where(jnp.abs(far_key - far_query - 4) > 1, 0.0, NEG) + has_right,
    ]
    for side in range(2):
        bias1[BLK * side : BLK * (side + 1)] = far_bias[side]

    def from_halo(pairs):
        units = [(pair, level, side) for pair in pairs for level in range(2) for side in range(2)]

        def place_of(level, side):
            which = (1 - level) if side == 0 else level
            return which, ((128, 512)[side] if level == 0 else OWN1)

        scores, mixings = [], []
        for pair, level, side in units:
            which, row = place_of(level, side)
            at = lanes(pair)
            scores.append(nn(kv[0, row : row + BLK, at], two_heads(halo_qg[side, 0, which, at, :])))
            mixings.append(nn(kv[1, row : row + BLK, at], two_heads(halo_qg[side, 1, which, at, :])))
        pieces = []
        for (pair, level, side), score, mixing in zip(units, scores, mixings):
            which, row = place_of(level, side)
            if level == 0:
                score = score + (has_left, has_right)[side]
            else:
                score = score + bias1[BLK * side : BLK * (side + 1)]
            weight = jnp.exp(score - pair_row(halo_stats.at[side, 0, which], pair))
            diff = weight * (mixing - pair_row(halo_stats.at[side, 1, which], pair))
            pieces.append((weight.astype(BF16), diff.astype(BF16)))
        parts = []
        for (pair, level, side), (weight, diff) in zip(units, pieces):
            which, row = place_of(level, side)
            at = lanes(pair)
            parts.append(
                (
                    nt(diff, two_heads(halo_qg[side, 0, which, at, :])),
                    nt(weight, two_heads(halo_qg[side, 1, which, at, :])),
                )
            )
        for (pair, level, side), both in zip(units, parts):
            which, row = place_of(level, side)
            at = lanes(pair)
            to = (row - 128) if level == 0 else 512
            for i in range(2):
                dkv[i, to : to + BLK, at] += both[i]

    from_halo(range(4))

    far_relay_across(2)

    def spread_rows(matrix, x):
        high, low = parts_of(x, 2)
        return nn(matrix, high) + nn(matrix, low)

    dkv[0, 0:ROWS] += spread_rows(pool1t[...], dkv[0, ROWS:] * 0.25)
    dkv[1, 0:ROWS] += spread_rows(pool1t[...], dkv[1, ROWS:])
    far_receive(1)
    far_receive(2)
    far_stats = g2win[:, FEAT:]
    stat_row = iota((BLK, 256), 0)
    same_head = (stat_row & 7) == (iota((BLK, 256), 1) >> 5)
    far_top = nn(far_stats, onehot(same_head & (stat_row < 24)))
    far_energy = nn(far_stats, onehot(same_head & (stat_row >= 24) & (stat_row < 48)))
    far_scores = nn(q2win[...], k2m[...]) + bias2[...]
    far_weight = jnp.exp(far_scores - far_top)
    far_mixing = nn(g2win[:, 0:FEAT], v2m[...])
    far_diff = (far_weight * (far_mixing - far_energy)).astype(BF16)
    lane_head = (iota((256, FEAT), 0) >> 5) == (iota((256, FEAT), 1) >> 6)
    dk2 = jnp.where(lane_head, nn(jnp.transpose(far_diff), q2win[...]), 0.0)
    dv2 = jnp.where(lane_head, nn(jnp.transpose(far_weight.astype(BF16)), g2win[:, 0:FEAT]), 0.0)

    key_grad = dkv[0, 0:ROWS] + spread_rows(pool2t[...], dk2 * (1.0 / 16))
    outputs[2] = key_grad.astype(BF16)
    store(2).start()
    value_grad = dkv[1, 0:ROWS] + spread_rows(pool2t[...], dv2)
    outputs[3] = value_grad.astype(BF16)
    store(3).start()

    for copies in (kv0_copy, kv1_copy, lambda side: qg_copy(side, 0), lambda side: qg_copy(side, 1), stats_copy):
        sent(copies)
    for phase in range(3):
        far_sent(phase)
    for i in range(4):
        store(i).wait()


def placing(order_any, held_any, out_ref, dq_ref, dk_ref, dv_ref, order_ref, held, results, in_sem, out_sem):
    targets = (out_ref, dq_ref, dk_ref, dv_ref)

    def load(i):
        return pltpu.make_async_copy(held_any.at[i], held.at[i], in_sem.at[i])

    def store(i):
        return pltpu.make_async_copy(results.at[i], targets[i], out_sem.at[i])

    order_load = pltpu.make_async_copy(order_any, order_ref, in_sem.at[4])
    order_load.start()
    for i in range(4):
        load(i).start()
    order_load.wait()
    order = order_ref[...] - lax.axis_index("seq") * ROWS
    place = onehot(iota((ROWS, ROWS), 0) == order)
    for i in range(4):
        load(i).wait()
        product = nt if i < 2 else nn
        results[i] = product(place, held[i]).astype(BF16)
        store(i).start()
    for i in range(4):
        store(i).wait()


def on_device(n, query_points, key_points, value_points, cotangent, hilbert_order):
    shape = jax.ShapeDtypeStruct((ROWS, FEAT), BF16)
    scratch = [
        ((1, ROWS), jnp.int32),
        ((4, ROWS, FEAT), BF16),
        ((4, ROWS, FEAT), BF16),
        ((BLK, ROWS), BF16),
        ((ROWS, BLK), BF16),
        ((256, ROWS), BF16),
        ((ROWS, 256), BF16),
        ((2, 1152, FEAT), BF16),
        ((2, FEAT, 1152), BF16),
        ((2, 32, FEAT), BF16),
        ((2, WIN2, FEAT), BF16),
        ((32, FEAT), BF16),
        ((WIN2, FEAT), BF16),
        ((2, FEAT, WIN2), BF16),
        ((2, 5, FEAT, BLK), BF16),
        ((2, 2, 2, FEAT, BLK), BF16),
        ((2, 5, HEADS, BLK), F32),
        ((2, 2, 2, HEADS, BLK), F32),
        ((FEAT, ROWS), BF16),
        ((5, 4, 384, 256), F32),
        ((5, HEADS, BLK), F32),
        ((5, FEAT, BLK), F32),
        ((FEAT, 256), BF16),
        ((FEAT, 256), BF16),
        ((FEAT, 256), BF16),
        ((FEAT, 256), BF16),
        ((WIN2, 256), F32),
        ((FEAT, 256), F32),
        ((32, 640), BF16),
        ((WIN2, 640), BF16),
        ((WIN2, 256), F32),
        ((WIN2, 256), F32),
        ((3, HEADS, ROWS), F32),
        ((HEADS, ROWS), F32),
        ((5, FEAT, BLK), F32),
        ((2, ROWS + BLK, FEAT), F32),
    ]
    anywhere = pl.BlockSpec(memory_space=pl.ANY)
    order = hilbert_order.reshape(1, ROWS)
    held = pl.pallas_call(
        functools.partial(kernel, n),
        out_shape=jax.ShapeDtypeStruct((4, ROWS, FEAT), BF16),
        in_specs=[pl.BlockSpec(memory_space=pltpu.HBM)] * 5,
        out_specs=anywhere,
        scratch_shapes=[pltpu.VMEM(dims, kind) for dims, kind in scratch]
        + [
            pltpu.SemaphoreType.DMA((2, 5)),
            pltpu.SemaphoreType.DMA((2, 5)),
            pltpu.SemaphoreType.DMA((3, 10)),
            pltpu.SemaphoreType.DMA((3, SLOTS)),
            pltpu.SemaphoreType.DMA((5,)),
            pltpu.SemaphoreType.DMA((4,)),
        ],
        compiler_params=pltpu.CompilerParams(
            collective_id=0, has_side_effects=True, vmem_limit_bytes=48 * 1024 * 1024
        ),
        cost_estimate=pl.CostEstimate(
            flops=8_000_000_000, bytes_accessed=4 * 1024 * 1024, transcendentals=2_500_000
        ),
    )(
        *[
            pltpu.with_memory_space_constraint(x, pltpu.HBM)
            for x in (order, query_points, key_points, value_points, cotangent)
        ]
    )
    return pl.pallas_call(
        placing,
        out_shape=(shape,) * 4,
        in_specs=[pl.BlockSpec(memory_space=pltpu.HBM), anywhere],
        out_specs=(anywhere,) * 4,
        scratch_shapes=[pltpu.VMEM((1, ROWS), jnp.int32)]
        + [pltpu.VMEM((4, ROWS, FEAT), BF16)] * 2
        + [pltpu.SemaphoreType.DMA((5,)), pltpu.SemaphoreType.DMA((4,))],
        compiler_params=pltpu.CompilerParams(vmem_limit_bytes=16 * 1024 * 1024),
        cost_estimate=pl.CostEstimate(
            flops=1_100_000_000, bytes_accessed=4 * 1024 * 1024, transcendentals=0
        ),
    )(pltpu.with_memory_space_constraint(order, pltpu.HBM), held)


def solution(mesh):
    return jax.shard_map(
        functools.partial(on_device, mesh.shape["seq"]),
        mesh=mesh,
        in_specs=(P("seq", None),) * 4 + (P("seq"),),
        out_specs=(P("seq", None),) * 4,
        check_vma=False,
    )
```

```python
import functools

import jax
import jax.numpy as jnp
from jax import lax
from jax.experimental import pallas as pl
from jax.experimental.pallas import tpu as pltpu
from jax.sharding import PartitionSpec as P

HEADS = 8
HEAD_DIM = 64
FEAT = 512
BLK = 128
ROWS = 512
SCALE = HEAD_DIM**-0.5
NEG = -1e30
MESH = pl.DeviceIdType.MESH
F32 = jnp.float32
BF16 = jnp.bfloat16

POS = {1: 0, 2: 1, 0: 2, 3: 4}
LEVEL1 = 3
WINDOW = {0: 128, 1: 256, 2: 0, 3: 768, 4: 384}
OWN1 = 768 + BLK
SLOTS = 10
WIN2 = 384


def nn(a, b):
    return lax.dot_general(a, b, (((1,), (0,)), ((), ())), preferred_element_type=F32)


def nt(a, b):
    return lax.dot_general(a, b, (((1,), (1,)), ((), ())), preferred_element_type=F32)


def iota(shape, dim):
    return lax.broadcasted_iota(jnp.int32, shape, dim)


def onehot(mask):
    return jnp.where(mask, 1.0, 0.0).astype(BF16)


def parts_of(x, count):
    parts = []
    for _ in range(count):
        part = x.astype(BF16)
        parts.append(part)
        x = x - part.astype(F32)
    return parts


def spread(x, matrix, count):
    total = None
    for part in parts_of(x, count):
        term = nn(part, matrix)
        total = term if total is None else total + term
    return total


def two_heads(x):
    zero = jnp.zeros((HEAD_DIM, x.shape[1]), x.dtype)
    upper = jnp.concatenate([x[:HEAD_DIM], zero], axis=1)
    lower = jnp.concatenate([zero, x[HEAD_DIM:]], axis=1)
    return jnp.concatenate([upper, lower], axis=0)


def own_blocks(x):
    return jnp.concatenate([x[:HEAD_DIM, :BLK], x[HEAD_DIM:, BLK:]], axis=0)


def kernel(
    n,
    order_any,
    q_any,
    k_any,
    v_any,
    dz_any,
    out_any,
    order_ref,
    inputs,
    outputs,
    pool1,
    pool1t,
    pool2,
    pool2t,
    kv,
    kvt,
    kv2own,
    kv2,
    q2own,
    q2win,
    kv2t,
    qg,
    halo_qg,
    stats,
    halo_stats,
    dzt,
    weights,
    sums,
    numer,
    q2m,
    g2m,
    k2m,
    v2m,
    weights2,
    numer2,
    g2own,
    g2win,
    bias1,
    bias2,
    share,
    delta,
    dqt,
    dkv,
    nb_send,
    nb_recv,
    l2_send,
    l2_recv,
    in_sem,
    out_sem,
):
    me = lax.axis_index("seq")
    left = lax.rem(me + n - 1, n)
    right = lax.rem(me + 1, n)
    core = lax.rem(me, 2)
    half = lax.rem(me // 2, 2)
    odd = lax.rem(me // 4, 2)
    base = 4 * (me // 4 - 1)
    sibling = me + 1 - 2 * core
    chips = [0, 1, 3 - half, 4, 5]
    inline = [2, 3 - 3 * odd, 4 - 3 * odd]
    across = [3 * odd, 1 + 3 * odd]
    peers = [base + 2 * chip + core for chip in (3 - half, 4 - 4 * odd, 5 - 4 * odd)]
    row_to = me + 8 - 16 * odd
    row_from = me - 8 + 16 * odd
    to_row = (row_to >= 0) & (row_to < n)
    from_row = (row_from >= 0) & (row_from < n)
    near = [me > 0, me < n - 1]

    barrier = pltpu.get_barrier_semaphore()

    def greet(device):
        pl.semaphore_signal(barrier, inc=1, device_id=(device,), device_id_type=MESH)

    for device in peers:
        greet(device)
    for device, there in ((left, near[0]), (right, near[1]), (row_to, to_row), (row_from, from_row)):
        pl.when(there)(functools.partial(greet, device))
    partners = 3 + sum(there.astype(jnp.int32) for there in near + [to_row, from_row])

    def load(i):
        return pltpu.make_async_copy((k_any, v_any, q_any, dz_any)[i], inputs.at[i], in_sem.at[i])

    def store(i):
        return pltpu.make_async_copy(outputs.at[i], out_any.at[i], out_sem.at[i])

    order_load = pltpu.make_async_copy(order_any, order_ref, in_sem.at[4])
    order_load.start()
    for i in range(4):
        load(i).start()

    def remote(src, dst, send, recv, device):
        return pltpu.make_async_remote_copy(
            src_ref=src,
            dst_ref=dst,
            send_sem=send,
            recv_sem=recv,
            device_id=(device,),
            device_id_type=MESH,
        )

    def kv0_copy(side):
        src, dst, to = [(512, 0, right), (128, 640, left)][side]
        return remote(
            kv.at[:, pl.ds(src, BLK)], kv.at[:, pl.ds(dst, BLK)],
            nb_send.at[side, 0], nb_recv.at[side, 0], to,
        )

    def kv1_copy(side):
        src, dst, to = [(OWN1, 768, right), (OWN1 + 32, 1056, left)][side]
        return remote(
            kv.at[:, pl.ds(src, 96)], kv.at[:, pl.ds(dst, 96)],
            nb_send.at[side, 1], nb_recv.at[side, 1], to,
        )

    def qg_copy(side, which):
        src, to = [(3, right), (2, left)][side]
        return remote(
            qg.at[which, pl.ds(src, 2)], halo_qg.at[side, which],
            nb_send.at[side, 2 + which], nb_recv.at[side, 2 + which], to,
        )

    def stats_copy(side):
        src, to = [(3, right), (2, left)][side]
        return remote(
            stats.at[:, pl.ds(src, 2)], halo_stats.at[side],
            nb_send.at[side, 4], nb_recv.at[side, 4], to,
        )

    def slot_rows(slot):
        return pl.ds(pl.multiple_of(32 * slot, 32), 32)

    def far_refs(phase, slot):
        if phase == 0:
            return kv2own, kv2.at[:, slot_rows(slot)]
        if phase == 1:
            return q2own, q2win.at[slot_rows(slot)]
        return g2own, g2win.at[slot_rows(slot)]

    def direct_copy(phase, i):
        slot = 2 * (2 if i == 0 else half + 3 * odd) + core
        src, dst = far_refs(phase, slot)
        return remote(src, dst, l2_send.at[phase, i], l2_recv.at[phase, slot], peers[i])

    def row_copy(phase, i):
        slot = 2 * across[i] + core
        _, src = far_refs(phase, 2 * inline[1 + i] + core)
        _, dst = far_refs(phase, slot)
        return remote(src, dst, l2_send.at[phase, 3 + i], l2_recv.at[phase, slot], row_to)

    def arrival(phase, slot):
        src, dst = far_refs(phase, slot)
        return remote(src, dst, l2_send.at[phase, 0], l2_recv.at[phase, slot], sibling)

    def relay_copy(phase, i):
        slot = 2 * (inline + across)[i] + core
        _, dst = far_refs(phase, slot)
        return remote(dst, dst, l2_send.at[phase, 5 + i], l2_recv.at[phase, slot], sibling)

    def send(copies):
        for side in range(2):
            pl.when(near[1 - side])(copies(side).start)

    def receive(copies):
        for side in range(2):
            pl.when(near[side])(copies(side).wait_recv)

    def sent(copies):
        for side in range(2):
            pl.when(near[1 - side])(copies(side).wait_send)

    def far_send(phase):
        for i in range(3):
            direct_copy(phase, i).start()

    def far_relay(phase):
        for i in (1, 2, 0):
            arrival(phase, 2 * inline[i] + core).wait_recv()
            if i:
                pl.when(to_row)(row_copy(phase, i - 1).start)
            relay_copy(phase, i).start()

    def far_relay_across(phase):
        for i in range(2):
            def step(i=i):
                arrival(phase, 2 * across[i] + core).wait_recv()
                relay_copy(phase, 3 + i).start()

            pl.when(from_row)(step)

    def far_receive(phase):
        for i in range(3):
            arrival(phase, 2 * inline[i] + 1 - core).wait_recv()
        for i in range(2):
            pl.when(from_row)(arrival(phase, 2 * across[i] + 1 - core).wait_recv)

    def far_sent(phase):
        for i in range(3):
            direct_copy(phase, i).wait_send()
            relay_copy(phase, i).wait_send()
        for i in range(2):
            pl.when(to_row)(row_copy(phase, i).wait_send)
            pl.when(from_row)(relay_copy(phase, 3 + i).wait_send)

    def clear(rows):
        for first in rows:
            kv[:, first : first + BLK] = jnp.zeros((2, BLK, FEAT), BF16)

    def clear_side(side):
        clear(((0, 768), (640, 1024))[side])
        halo_qg[side] = jnp.zeros((2, 2, FEAT, BLK), BF16)
        halo_stats[side] = jnp.zeros((2, 2, HEADS, BLK), F32)

    def clear_far(first):
        kv2[:, first : first + 128] = jnp.zeros((2, 128, FEAT), BF16)
        q2win[first : first + 128] = jnp.zeros((128, FEAT), BF16)
        g2win[first : first + 128] = jnp.zeros((128, 640), BF16)

    order_load.wait()
    order = order_ref[...] - me * ROWS
    column = jnp.transpose(jnp.broadcast_to(order.astype(F32), (BLK, ROWS)))
    lane = iota((ROWS, BLK), 1).astype(F32)
    gather = jnp.concatenate(
        [jnp.where(column == lane + float(BLK * i), 1.0, 0.0).astype(BF16) for i in range(4)], axis=1
    )

    pool2[...] = onehot((iota((256, ROWS), 0) & 31) == (iota((256, ROWS), 1) >> 4))

    for which in range(2):
        load(which).wait()
        kv[which, 128:640] = nn(gather, inputs[which]).astype(BF16)
    kv2own[0] = (nn(pool2[0:32], kv[0, 128:640]) * (1.0 / 16)).astype(BF16)
    kv2own[1] = nn(pool2[0:32], kv[1, 128:640]).astype(BF16)
    pl.semaphore_wait(barrier, partners)
    far_send(0)
    send(kv0_copy)
    pool1[...] = onehot(iota((BLK, ROWS), 0) == (iota((BLK, ROWS), 1) >> 2))
    kv[0, OWN1 : OWN1 + BLK] = (nn(pool1[...], kv[0, 128:640]) * 0.25).astype(BF16)
    kv[1, OWN1 : OWN1 + BLK] = nn(pool1[...], kv[1, 128:640]).astype(BF16)
    send(kv1_copy)
    pool1t[...] = onehot((iota((ROWS, BLK), 0) >> 2) == iota((ROWS, BLK), 1))
    pool2t[...] = onehot((iota((ROWS, 256), 0) >> 4) == (iota((ROWS, 256), 1) & 31))

    for side in range(2):
        pl.when(jnp.logical_not(near[side]))(functools.partial(clear_side, side))
    pl.when(me < 4)(functools.partial(clear_far, 0))
    pl.when(me >= n - 4)(functools.partial(clear_far, 192))
    kv2[:, 320:384] = jnp.zeros((2, 64, FEAT), BF16)
    q2win[320:384] = jnp.zeros((64, FEAT), BF16)
    g2win[320:384] = jnp.zeros((64, 640), BF16)

    load(2).wait()
    query = (nn(gather, inputs[2]) * SCALE).astype(BF16)
    q2own[...] = (nn(pool2[0:32], query) * (1.0 / 16)).astype(BF16)
    query_t = jnp.transpose(query)
    for b in range(4):
        qg[0, POS[b]] = query_t[:, BLK * b : BLK * (b + 1)]
    qg[0, LEVEL1] = (nn(query_t, pool1t[...]) * 0.25).astype(BF16)

    head_lane = (iota((FEAT, 256), 0) >> 6) == (iota((FEAT, 256), 1) >> 5)
    q2m[...] = jnp.where(head_lane, nn(query_t, pool2t[...]) * (1.0 / 16), 0.0).astype(BF16)
    kvt[0, :, 128:640] = jnp.transpose(kv[0, 128:640])
    kvt[1, :, 128:640] = jnp.transpose(kv[1, 128:640])
    load(3).wait()
    dzt[...] = jnp.transpose(nn(gather, inputs[3]).astype(BF16))
    k2m[...] = jnp.where(
        head_lane, nn(kvt[0, :, 128:640], pool2t[...]) * (1.0 / 16), 0.0
    ).astype(BF16)
    v2m[...] = jnp.where(head_lane, nn(kvt[1, :, 128:640], pool2t[...]), 0.0).astype(BF16)

    has_left = jnp.where(me > 0, 0.0, NEG).astype(F32)
    has_right = jnp.where(me < n - 1, 0.0, NEG).astype(F32)
    key_sub = (iota((WIN2, 256), 0) >> 5) - 4
    query_sub = (iota((WIN2, 256), 1) & 127) >> 5
    apart = jnp.where(jnp.abs(key_sub - query_sub) > 1, 0.0, NEG)
    bias1[0:BLK] = apart[0:BLK] + has_left
    bias1[BLK : 2 * BLK] = apart[BLK : 2 * BLK]
    bias1[2 * BLK :] = apart[2 * BLK :] + has_right
    for slot in range(12):
        if slot < SLOTS:
            device = base + 2 * chips[slot // 2] + slot % 2
            valid = (device >= 0) & (device < n) & (jnp.abs(device - me) > 1)
            level = jnp.where(valid, 0.0, NEG).astype(F32)
        else:
            level = jnp.float32(NEG)
        bias2[32 * slot : 32 * slot + 32] = jnp.zeros((32, 256), F32) + level

    def lanes(pair):
        return slice(BLK * pair, BLK * (pair + 1))

    def head_rows(head):
        return slice(HEAD_DIM * head, HEAD_DIM * (head + 1))

    def forward_scores(pair, pos):
        at = lanes(pair)
        start = WINDOW[pos]
        return nn(kv[0, start : start + 384, at], two_heads(qg[0, pos, at, :]))

    def forward_weights(pair, pos, raw):
        pieces = [raw[BLK * i : BLK * (i + 1)] for i in range(3)]
        if pos == POS[0]:
            pieces[0] = pieces[0] + has_left
        if pos == POS[3]:
            pieces[2] = pieces[2] + has_right
        if pos == LEVEL1:
            pieces = [piece + bias1[BLK * i : BLK * (i + 1)] for i, piece in enumerate(pieces)]
        top = jnp.max(jnp.maximum(jnp.maximum(pieces[0], pieces[1]), pieces[2]), axis=0, keepdims=True)
        total = None
        rounded = []
        for i, piece in enumerate(pieces):
            piece = jnp.exp(piece - top)
            weights[pos, pair, BLK * i : BLK * (i + 1)] = piece
            total = piece if total is None else total + piece
            rounded.append(piece.astype(BF16))
        total = jnp.sum(total, axis=0, keepdims=True) * (4.0 if pos == LEVEL1 else 1.0)
        for e in range(2):
            stats[0, pos, pl.ds(2 * pair + e, 1), :] = top[:, BLK * e : BLK * (e + 1)]
            sums[pos, pl.ds(2 * pair + e, 1), :] = total[:, BLK * e : BLK * (e + 1)]
        return jnp.concatenate(rounded, axis=0)

    def forward_mix(pair, pos, rounded):
        at = lanes(pair)
        start = WINDOW[pos]
        numer[pos, at, :] = own_blocks(nn(kvt[1, at, start : start + 384], rounded))

    def forward_all(units):
        raws = [forward_scores(*unit) for unit in units]
        rounded = [forward_weights(*unit, raw) for unit, raw in zip(units, raws)]
        for unit, value in zip(units, rounded):
            forward_mix(*unit, value)

    def forward_inner(pairs):
        forward_all([(pair, pos) for pair in pairs for pos in (0, 1)])

    forward_inner(range(4))

    far_relay(0)
    receive(kv0_copy)
    for which in range(2):
        scale = 0.25 if which == 0 else 1.0
        for source, target in ((0, 864), (640, 1024)):
            pooled = nn(pool1[0:32, 0:BLK], kv[which, source : source + BLK])
            kv[which, target : target + 32] = (pooled * scale).astype(BF16)
    receive(kv1_copy)
    send(lambda side: qg_copy(side, 0))
    far_send(1)
    far_relay_across(0)
    for which in range(2):
        kvt[which, :, 0:128] = jnp.transpose(kv[which, 0:128])
        kvt[which, :, 640:1152] = jnp.transpose(kv[which, 640:1152])

    def forward_rim(pairs):
        forward_all([(pair, pos) for pair in pairs for pos in (2, 4, 3)])

    forward_rim(range(4))

    far_receive(0)
    for which in range(2):
        kv2t[which] = jnp.transpose(kv2[which])
    scores = nn(kv2[0], q2m[...]) + bias2[...]
    top2 = jnp.max(scores, axis=0, keepdims=True)
    scores = jnp.exp(scores - top2)
    weights2[...] = scores
    total2 = jnp.sum(scores, axis=0, keepdims=True) * 16.0
    numer2[...] = jnp.where(head_lane, nn(kv2t[1], scores.astype(BF16)), 0.0)

    def by_block(ref):
        return jnp.concatenate([ref[POS[b]] for b in range(4)], axis=1)

    head_row = iota((HEADS, 256), 0) == (iota((HEADS, 256), 1) >> 5)

    def rows2(x):
        return jnp.where(head_row, jnp.broadcast_to(x, (HEADS, 256)), 0.0)

    tops = [
        by_block(stats.at[0]),
        spread(stats[0, LEVEL1], pool1[...], 3),
        spread(rows2(top2), pool2[...], 3),
    ]
    totals = [
        by_block(sums),
        spread(sums[LEVEL1], pool1[...], 3),
        spread(rows2(total2), pool2[...], 3),
    ]
    best = jnp.maximum(jnp.maximum(tops[0], tops[1]), tops[2])
    scales = [jnp.exp(top - best) for top in tops]
    denom = scales[0] * totals[0] + scales[1] * totals[1] + scales[2] * totals[2]
    for level in range(3):
        share[level] = scales[level] / denom

    def combine(pairs):
        spreads = []
        for pair in pairs:
            at = lanes(pair)
            spreads.append((spread(numer[LEVEL1, at, :], pool1[...], 2), spread(numer2[at, :], pool2[...], 2)))
        scaled = []
        for pair, (middle, coarse) in zip(pairs, spreads):
            at = lanes(pair)
            fine = jnp.concatenate([numer[POS[b], at, :] for b in range(4)], axis=1)
            grads = dzt[at, :].astype(F32)
            for e in range(2):
                head = 2 * pair + e
                cut = slice(HEAD_DIM * e, HEAD_DIM * (e + 1))
                to = head_rows(head)
                parts = [share[level, pl.ds(head, 1), :] for level in range(3)]
                grad = grads[cut]
                value = parts[0] * fine[cut] + parts[1] * middle[cut] + parts[2] * coarse[cut]
                outputs[0, to, :] = value.astype(BF16)
                delta[pl.ds(head, 1), :] = jnp.sum(grad * value, axis=0, keepdims=True)
                own = (parts[0] * grad).astype(BF16)
                for b in range(4):
                    qg[1, POS[b], to, :] = own[:, BLK * b : BLK * (b + 1)]
                scaled.append((head, parts_of(parts[1] * grad, 2), parts_of(parts[2] * grad, 2)))
        for head, middle, coarse in scaled:
            to = head_rows(head)
            qg[1, LEVEL1, to, :] = (nn(middle[0], pool1t[...]) + nn(middle[1], pool1t[...])).astype(BF16)
            pooled = nn(coarse[0], pool2t[...]) + nn(coarse[1], pool2t[...])
            keep = (iota((HEAD_DIM, 256), 1) >> 5) == head
            g2m[to, :] = jnp.where(keep, pooled, 0.0).astype(BF16)

    combine(range(4))
    store(0).start()

    energy = share[0] * delta[...]
    for b in range(4):
        stats[1, POS[b]] = energy[:, BLK * b : BLK * (b + 1)]
    stats[1, LEVEL1] = spread(share[1] * delta[...], pool1t[...], 3) * 4.0
    energy2 = jnp.sum(
        jnp.where(head_row, spread(share[2] * delta[...], pool2t[...], 3), 0.0), axis=0, keepdims=True
    ) * 16.0

    pick = iota((32, 256), 0) == (iota((32, 256), 1) & 31)
    g2own[:, 0:FEAT] = nt(onehot(pick), g2m[...]).astype(BF16)
    packed = None
    for i, part in enumerate(parts_of(top2, 3) + parts_of(energy2, 3)):
        chosen = jnp.where(pick, jnp.broadcast_to(part.astype(F32), (32, 256)), 0.0).astype(BF16)
        target = onehot(iota((256, BLK), 1) == (iota((256, BLK), 0) >> 5) + 8 * i)
        term = nn(chosen, target)
        packed = term if packed is None else packed + term
    g2own[:, FEAT:] = packed.astype(BF16)
    far_send(2)
    send(stats_copy)
    send(lambda side: qg_copy(side, 1))
    far_relay(1)

    def pair_row(ref, pair):
        return jnp.concatenate([ref[pl.ds(2 * pair + e, 1), :] for e in range(2)], axis=1)

    def backward(pairs):
        sums_of = [({}, {}) for pair in pairs]

        def mixing_of(pair, pos):
            at = lanes(pair)
            start = WINDOW[pos]
            return nn(kv[1, start : start + 384, at], two_heads(qg[1, pos, at, :]))

        def diff_of(pair, pos, mixing):
            return (weights[pos, pair] * (mixing - pair_row(stats.at[1, pos], pair))).astype(BF16)

        def grads_of(sums_here, pair, pos, diff):
            at = lanes(pair)
            start = WINDOW[pos]
            query_m = two_heads(qg[0, pos, at, :])
            grad_m = two_heads(qg[1, pos, at, :])
            dqt[pos, at, :] = own_blocks(nn(kvt[0, at, start : start + 384], diff))
            own = [i for i in range(3) if 128 <= start + BLK * i < 640 or start + BLK * i == OWN1]
            rows = slice(BLK * own[0], BLK * (own[-1] + 1))
            key_part = nt(diff[rows], query_m)
            value_part = nt(weights[pos, pair, rows].astype(BF16), grad_m)
            for i in own:
                block = (start + BLK * i - 128) // BLK if pos != LEVEL1 else 4
                cut = slice(BLK * (i - own[0]), BLK * (i - own[0] + 1))
                for held, part in zip(sums_here, (key_part, value_part)):
                    held[block] = part[cut] if block not in held else held[block] + part[cut]
            if pos == 4:
                for which in range(2):
                    for block in range(5):
                        dkv[which, BLK * block : BLK * (block + 1), at] = sums_here[which][block]

        units = [(pair, pos) for pair in pairs for pos in range(5)]
        mixings = [mixing_of(*unit) for unit in units]
        diffs = [diff_of(*unit, mixing) for unit, mixing in zip(units, mixings)]
        for i, (unit, diff) in enumerate(zip(units, diffs)):
            grads_of(sums_of[i // 5], *unit, diff)

    backward(range(4))
    far_relay(2)
    far_relay_across(1)

    mixing2 = nn(kv2[1], g2m[...])
    diff2 = (weights2[...] * (mixing2 - energy2)).astype(BF16)
    dq2 = jnp.where(head_lane, nn(kv2t[0], diff2), 0.0)
    query_grad = jnp.concatenate([dqt[POS[b]] for b in range(4)], axis=1)
    query_grad = query_grad + spread(dqt[LEVEL1] * 0.25, pool1[...], 2)
    query_grad = (query_grad + spread(dq2 * (1.0 / 16), pool2[...], 2)) * SCALE
    outputs[1] = query_grad.astype(BF16)
    store(1).start()

    receive(lambda side: qg_copy(side, 0))
    receive(stats_copy)
    receive(lambda side: qg_copy(side, 1))

    far_query = (iota((BLK, 256), 1) & 127) >> 5
    far_key = iota((BLK, 256), 0) >> 5
    far_bias = [
        jnp.where(jnp.abs(far_key - far_query + 4) > 1, 0.0, NEG) + has_left,
        jnp.where(jnp.abs(far_key - far_query - 4) > 1, 0.0, NEG) + has_right,
    ]
    for side in range(2):
        bias1[BLK * side : BLK * (side + 1)] = far_bias[side]

    def from_halo(pairs):
        units = [(pair, level, side) for pair in pairs for level in range(2) for side in range(2)]

        def place_of(level, side):
            which = (1 - level) if side == 0 else level
            return which, ((128, 512)[side] if level == 0 else OWN1)

        scores, mixings = [], []
        for pair, level, side in units:
            which, row = place_of(level, side)
            at = lanes(pair)
            scores.append(nn(kv[0, row : row + BLK, at], two_heads(halo_qg[side, 0, which, at, :])))
            mixings.append(nn(kv[1, row : row + BLK, at], two_heads(halo_qg[side, 1, which, at, :])))
        pieces = []
        for (pair, level, side), score, mixing in zip(units, scores, mixings):
            which, row = place_of(level, side)
            if level == 0:
                score = score + (has_left, has_right)[side]
            else:
                score = score + bias1[BLK * side : BLK * (side + 1)]
            weight = jnp.exp(score - pair_row(halo_stats.at[side, 0, which], pair))
            diff = weight * (mixing - pair_row(halo_stats.at[side, 1, which], pair))
            pieces.append((weight.astype(BF16), diff.astype(BF16)))
        parts = []
        for (pair, level, side), (weight, diff) in zip(units, pieces):
            which, row = place_of(level, side)
            at = lanes(pair)
            parts.append(
                (
                    nt(diff, two_heads(halo_qg[side, 0, which, at, :])),
                    nt(weight, two_heads(halo_qg[side, 1, which, at, :])),
                )
            )
        for (pair, level, side), both in zip(units, parts):
            which, row = place_of(level, side)
            at = lanes(pair)
            to = (row - 128) if level == 0 else 512
            for i in range(2):
                dkv[i, to : to + BLK, at] += both[i]

    from_halo(range(4))

    far_relay_across(2)

    def spread_rows(matrix, x):
        high, low = parts_of(x, 2)
        return nn(matrix, high) + nn(matrix, low)

    dkv[0, 0:ROWS] += spread_rows(pool1t[...], dkv[0, ROWS:] * 0.25)
    dkv[1, 0:ROWS] += spread_rows(pool1t[...], dkv[1, ROWS:])
    far_receive(1)
    far_receive(2)
    far_stats = g2win[:, FEAT:]
    stat_row = iota((BLK, 256), 0)
    same_head = (stat_row & 7) == (iota((BLK, 256), 1) >> 5)
    far_top = nn(far_stats, onehot(same_head & (stat_row < 24)))
    far_energy = nn(far_stats, onehot(same_head & (stat_row >= 24) & (stat_row < 48)))
    far_scores = nn(q2win[...], k2m[...]) + bias2[...]
    far_weight = jnp.exp(far_scores - far_top)
    far_mixing = nn(g2win[:, 0:FEAT], v2m[...])
    far_diff = (far_weight * (far_mixing - far_energy)).astype(BF16)
    lane_head = (iota((256, FEAT), 0) >> 5) == (iota((256, FEAT), 1) >> 6)
    dk2 = jnp.where(lane_head, nn(jnp.transpose(far_diff), q2win[...]), 0.0)
    dv2 = jnp.where(lane_head, nn(jnp.transpose(far_weight.astype(BF16)), g2win[:, 0:FEAT]), 0.0)

    key_grad = dkv[0, 0:ROWS] + spread_rows(pool2t[...], dk2 * (1.0 / 16))
    outputs[2] = key_grad.astype(BF16)
    store(2).start()
    value_grad = dkv[1, 0:ROWS] + spread_rows(pool2t[...], dv2)
    outputs[3] = value_grad.astype(BF16)
    store(3).start()

    for copies in (kv0_copy, kv1_copy, lambda side: qg_copy(side, 0), lambda side: qg_copy(side, 1), stats_copy):
        sent(copies)
    for phase in range(3):
        far_sent(phase)
    for i in range(4):
        store(i).wait()


def placing(order_any, held, out_ref, dq_ref, dk_ref, dv_ref, order_ref, results, in_sem, out_sem):
    targets = (out_ref, dq_ref, dk_ref, dv_ref)

    def store(i):
        return pltpu.make_async_copy(results.at[i], targets[i], out_sem.at[i])

    order_load = pltpu.make_async_copy(order_any, order_ref, in_sem.at[0])
    order_load.start()
    order_load.wait()
    order = order_ref[...] - lax.axis_index("seq") * ROWS
    place = onehot(iota((ROWS, ROWS), 0) == order)
    for i in range(4):
        product = nt if i < 2 else nn
        results[i] = product(place, held[i]).astype(BF16)
        store(i).start()
    for i in range(4):
        store(i).wait()


def on_device(n, query_points, key_points, value_points, cotangent, hilbert_order):
    shape = jax.ShapeDtypeStruct((ROWS, FEAT), BF16)
    scratch = [
        ((1, ROWS), jnp.int32),
        ((4, ROWS, FEAT), BF16),
        ((4, ROWS, FEAT), BF16),
        ((BLK, ROWS), BF16),
        ((ROWS, BLK), BF16),
        ((256, ROWS), BF16),
        ((ROWS, 256), BF16),
        ((2, 1152, FEAT), BF16),
        ((2, FEAT, 1152), BF16),
        ((2, 32, FEAT), BF16),
        ((2, WIN2, FEAT), BF16),
        ((32, FEAT), BF16),
        ((WIN2, FEAT), BF16),
        ((2, FEAT, WIN2), BF16),
        ((2, 5, FEAT, BLK), BF16),
        ((2, 2, 2, FEAT, BLK), BF16),
        ((2, 5, HEADS, BLK), F32),
        ((2, 2, 2, HEADS, BLK), F32),
        ((FEAT, ROWS), BF16),
        ((5, 4, 384, 256), F32),
        ((5, HEADS, BLK), F32),
        ((5, FEAT, BLK), F32),
        ((FEAT, 256), BF16),
        ((FEAT, 256), BF16),
        ((FEAT, 256), BF16),
        ((FEAT, 256), BF16),
        ((WIN2, 256), F32),
        ((FEAT, 256), F32),
        ((32, 640), BF16),
        ((WIN2, 640), BF16),
        ((WIN2, 256), F32),
        ((WIN2, 256), F32),
        ((3, HEADS, ROWS), F32),
        ((HEADS, ROWS), F32),
        ((5, FEAT, BLK), F32),
        ((2, ROWS + BLK, FEAT), F32),
    ]
    anywhere = pl.BlockSpec(memory_space=pl.ANY)
    order = hilbert_order.reshape(1, ROWS)
    held = pl.pallas_call(
        functools.partial(kernel, n),
        out_shape=jax.ShapeDtypeStruct((4, ROWS, FEAT), BF16),
        in_specs=[pl.BlockSpec(memory_space=pltpu.HBM)] * 5,
        out_specs=anywhere,
        scratch_shapes=[pltpu.VMEM(dims, kind) for dims, kind in scratch]
        + [
            pltpu.SemaphoreType.DMA((2, 5)),
            pltpu.SemaphoreType.DMA((2, 5)),
            pltpu.SemaphoreType.DMA((3, 10)),
            pltpu.SemaphoreType.DMA((3, SLOTS)),
            pltpu.SemaphoreType.DMA((5,)),
            pltpu.SemaphoreType.DMA((4,)),
        ],
        compiler_params=pltpu.CompilerParams(
            collective_id=0, has_side_effects=True, vmem_limit_bytes=48 * 1024 * 1024
        ),
        cost_estimate=pl.CostEstimate(
            flops=8_000_000_000, bytes_accessed=4 * 1024 * 1024, transcendentals=2_500_000
        ),
    )(
        *[
            pltpu.with_memory_space_constraint(x, pltpu.HBM)
            for x in (order, query_points, key_points, value_points, cotangent)
        ]
    )
    return pl.pallas_call(
        placing,
        out_shape=(shape,) * 4,
        in_specs=[pl.BlockSpec(memory_space=pltpu.HBM), pl.BlockSpec(memory_space=pltpu.VMEM)],
        out_specs=(anywhere,) * 4,
        scratch_shapes=[pltpu.VMEM((1, ROWS), jnp.int32)]
        + [pltpu.VMEM((4, ROWS, FEAT), BF16)]
        + [pltpu.SemaphoreType.DMA((1,)), pltpu.SemaphoreType.DMA((4,))],
        compiler_params=pltpu.CompilerParams(vmem_limit_bytes=16 * 1024 * 1024),
        cost_estimate=pl.CostEstimate(
            flops=1_100_000_000, bytes_accessed=4 * 1024 * 1024, transcendentals=0
        ),
    )(pltpu.with_memory_space_constraint(order, pltpu.HBM), held)


def solution(mesh):
    return jax.shard_map(
        functools.partial(on_device, mesh.shape["seq"]),
        mesh=mesh,
        in_specs=(P("seq", None),) * 4 + (P("seq"),),
        out_specs=(P("seq", None),) * 4,
        check_vma=False,
    )
```
